32 devices in a mesh: shard: 8 (over z, y), tensor: 4 (over x, core).
Axes of the slice: x: 2, y: 2, z: 4, core: 2. Of those that a mesh axis runs over, the one named last changes fastest.
Arguments:
- attn_weight: float32 [4, 2048, 2048], P(None, 'shard', 'tensor'), may hold values from -62 to 62
- ffin_weight: float32 [2, 2048, 5120], P(None, 'shard', 'tensor'), may hold values from -62 to 62
- ffout_weight: float32 [1, 5120, 2048], P(None, 'shard', 'tensor'), may hold values from -62 to 62
- attn_grad: float32 [4, 2048, 2048], P(None, 'shard', 'tensor'), may hold values from -62 to 62
- ffin_grad: float32 [2, 2048, 5120], P(None, 'shard', 'tensor'), may hold values from -62 to 62
- ffout_grad: float32 [1, 5120, 2048], P(None, 'shard', 'tensor'), may hold values from -62 to 62
- attn_first: float32 [4, 2048, 2048], P(None, ('shard', 'tensor')), may hold values from -62 to 62
- ffin_first: float32 [2, 5120, 2048], P(None, ('shard', 'tensor')), may hold values from -62 to 62
- ffout_first: float32 [1, 2048, 5120], P(None, ('shard', 'tensor')), may hold values from -62 to 62
- attn_second: float32 [4, 2048, 2048], P(None, ('shard', 'tensor')), may hold values from 0.01 to 1
- ffin_second: float32 [2, 5120, 2048], P(None, ('shard', 'tensor')), may hold values from 0.01 to 1
- ffout_second: float32 [1, 2048, 5120], P(None, ('shard', 'tensor')), may hold values from 0.01 to 1
Outputs:
- attn_new: float32 [4, 2048, 2048], P(None, 'shard', 'tensor')
- ffin_new: float32 [2, 2048, 5120], P(None, 'shard', 'tensor')
- ffout_new: float32 [1, 5120, 2048], P(None, 'shard', 'tensor')
- attn_first_new: float32 [4, 2048, 2048], P(None, ('shard', 'tensor'))
- ffin_first_new: float32 [2, 5120, 2048], P(None, ('shard', 'tensor'))
- ffout_first_new: float32 [1, 2048, 5120], P(None, ('shard', 'tensor'))
- attn_second_new: float32 [4, 2048, 2048], P(None, ('shard', 'tensor'))
- ffin_second_new: float32 [2, 5120, 2048], P(None, ('shard', 'tensor'))
- ffout_second_new: float32 [1, 2048, 5120], P(None, ('shard', 'tensor'))
- trust_ratio: float32 [7], replicated
The draws below stay inside these ranges and needn't reach their ends.
All inputs are finite; a program needn't handle non-finite values.
Results may differ from the reference program's by a relative error of at most 0.00002.
Values sent between devices are 32-bit elements; how exact they have to be, the bound alone decides.
A program may use at most 128 MiB of HBM per device.

```python
import math
import jax
import jax.numpy as jnp
from jax import lax

D = 2048
FF = 5120


def rough_field(key, shape, row_dim, col_dim):
    key_base, key_rows, key_cols = jax.random.split(key, 3)
    base = jnp.clip(jax.random.normal(key_base, shape, jnp.float32), -6.0, 6.0)
    row_count = shape[row_dim]
    col_count = shape[col_dim]
    row_scale = 10.0 ** (0.5 * jax.random.uniform(key_rows, (row_count,), jnp.float32) - 0.25)
    row_scale = row_scale * (1.0 + 0.8 * jnp.arange(row_count, dtype=jnp.float32) / row_count)
    col_scale = 10.0 ** (0.5 * jax.random.uniform(key_cols, (col_count,), jnp.float32) - 0.25)
    col_scale = col_scale * (1.0 + 0.8 * jnp.arange(col_count, dtype=jnp.float32) / col_count)
    row_shape = [1] * len(shape)
    row_shape[row_dim] = row_count
    col_shape = [1] * len(shape)
    col_shape[col_dim] = col_count
    return base * row_scale.reshape(row_shape) * col_scale.reshape(col_shape)


def draw_attn_weight(key, part):
    return rough_field(jax.random.fold_in(key, 11), (4, D, D), 1, 2)


def draw_ffin_weight(key, part):
    return rough_field(jax.random.fold_in(key, 12), (2, D, FF), 1, 2)


def draw_ffout_weight(key, part):
    return rough_field(jax.random.fold_in(key, 13), (1, FF, D), 1, 2)


def draw_attn_grad(key, part):
    return rough_field(jax.random.fold_in(key, 21), (4, D, D), 1, 2)


def draw_ffin_grad(key, part):
    return rough_field(jax.random.fold_in(key, 22), (2, D, FF), 1, 2)


def draw_ffout_grad(key, part):
    return rough_field(jax.random.fold_in(key, 23), (1, FF, D), 1, 2)


def draw_attn_first(key, part):
    return rough_field(jax.random.fold_in(key, 31), (4, D, D), 2, 1)


def draw_ffin_first(key, part):
    return rough_field(jax.random.fold_in(key, 32), (2, FF, D), 2, 1)


def draw_ffout_first(key, part):
    return rough_field(jax.random.fold_in(key, 33), (1, D, FF), 2, 1)


def block_levels(stream_key, dims, pieces, low, largest):
    def one(axis_at, parts):
        draws = jax.random.uniform(jax.random.fold_in(jax.random.fold_in(stream_key, 6), axis_at), (parts,), jnp.float32, low / len(pieces), largest / len(pieces))
        return jnp.repeat(jnp.exp(draws), dims[axis_at] // parts).reshape((-1,) + (1,) * (len(dims) - axis_at - 1))

    gain = one(*pieces[0])
    for cut in pieces[1:]:
        gain = gain * one(*cut)
    return gain


def setup_inputs(seed: int = 0) -> dict:
    streams_of = jax.random.split(jax.random.key(seed), 13)
    attn_weight = draw_attn_weight(jax.random.fold_in(streams_of[12], 71), 0)
    ffin_weight = draw_ffin_weight(jax.random.fold_in(streams_of[12], 71), 0)
    ffout_weight = draw_ffout_weight(jax.random.fold_in(streams_of[12], 71), 0)
    attn_grad = draw_attn_grad(jax.random.fold_in(streams_of[12], 71), 0)
    ffin_grad = draw_ffin_grad(jax.random.fold_in(streams_of[12], 71), 0)
    ffout_grad = draw_ffout_grad(jax.random.fold_in(streams_of[12], 71), 0)
    attn_first = draw_attn_first(jax.random.fold_in(streams_of[12], 71), 0)
    ffin_first = draw_ffin_first(jax.random.fold_in(streams_of[12], 71), 0)
    ffout_first = draw_ffout_first(jax.random.fold_in(streams_of[12], 71), 0)
    attn_second = jnp.clip(jnp.exp(math.log(1.0) - 4.6051702 * jax.random.uniform(streams_of[9], (4, D, D), jnp.float32) ** block_levels(streams_of[9], (4, D, D), ((1, 32),), -0.2, 0.2)), 0.01, 1.0)
    ffin_second = jnp.clip(jnp.exp(math.log(1.0) - 4.6051702 * jax.random.uniform(streams_of[10], (2, FF, D), jnp.float32) ** block_levels(streams_of[10], (2, FF, D), ((1, 32),), -0.2, 0.2)), 0.01, 1.0)
    ffout_second = jnp.clip(jnp.exp(math.log(1.0) - 4.6051702 * jax.random.uniform(streams_of[11], (1, D, FF), jnp.float32) ** block_levels(streams_of[11], (1, D, FF), ((1, 32),), -0.2, 0.2)), 0.01, 1.0)
    return {"attn_weight": attn_weight, "ffin_weight": ffin_weight, "ffout_weight": ffout_weight, "attn_grad": attn_grad, "ffin_grad": ffin_grad, "ffout_grad": ffout_grad, "attn_first": attn_first, "ffin_first": ffin_first, "ffout_first": ffout_first, "attn_second": attn_second, "ffin_second": ffin_second, "ffout_second": ffout_second}


beta_one = 0.9
beta_two = 0.999
step_number = 10.0
correct_one = 1.0 - beta_one ** step_number
correct_two = 1.0 - beta_two ** step_number
learn_rate = 0.02
decay_rate = 0.1
epsilon = 1e-06

def moment_step(gradient_t, first_moment, second):
    first_new = beta_one * first_moment + (1.0 - beta_one) * gradient_t
    second_new = beta_two * second + (1.0 - beta_two) * gradient_t * gradient_t
    ratio_value = first_new / correct_one / (jnp.sqrt(second_new / correct_two) + epsilon)
    return (first_new, second_new, ratio_value)

def reference(attn_weight, ffin_weight, ffout_weight, attn_grad, ffin_grad, ffout_grad, attn_first, ffin_first, ffout_first, attn_second, ffin_second, ffout_second):
    weights = (attn_weight, ffin_weight, ffout_weight)
    gradients = (attn_grad, ffin_grad, ffout_grad)
    firsts = (attn_first, ffin_first, ffout_first)
    seconds = (attn_second, ffin_second, ffout_second)
    results = [moment_step(jnp.swapaxes(gradients[position], 1, 2), firsts[position], seconds[position]) for position in range(3)]
    updates = [jnp.swapaxes(results[position][2], 1, 2) + decay_rate * weights[position] for position in range(3)]
    weight_sq = jnp.concatenate([lax.optimization_barrier(jnp.sum(matrix * matrix, axis=(1, 2))) for matrix in weights])
    update_sq = jnp.concatenate([lax.optimization_barrier(jnp.sum(member * member, axis=(1, 2))) for member in updates])
    trust_ratio = jnp.sqrt(weight_sq) / (jnp.sqrt(update_sq) + epsilon)
    scales = (trust_ratio[0:4], trust_ratio[4:6], trust_ratio[6:7])
    new_weights = [weights[position] - learn_rate * scales[position][:, None, None] * updates[position] for position in range(3)]
    return (new_weights[0], new_weights[1], new_weights[2], results[0][0], results[1][0], results[2][0], results[0][1], results[1][1], results[2][1], trust_ratio)
```

```python
import functools

import jax
import jax.numpy as jnp
from jax import lax
from jax.experimental import pallas as pl
from jax.experimental.pallas import tpu as pltpu
from jax.sharding import PartitionSpec as P

MESH = pl.DeviceIdType.MESH
RELAY_OUT = False
RELAY_BACK = False

beta_one = 0.9
beta_two = 0.999
step_number = 10.0
correct_one = 1.0 - beta_one**step_number
correct_two = 1.0 - beta_two**step_number
learn_rate = 0.02
decay_rate = 0.1
epsilon = 1e-06


def moment_step(gradient_t, first_moment, second):
    first_new = beta_one * first_moment + (1.0 - beta_one) * gradient_t
    second_new = beta_two * second + (1.0 - beta_two) * gradient_t * gradient_t
    ratio_value = first_new / correct_one / (jnp.sqrt(second_new / correct_two) + epsilon)
    return (first_new, second_new, ratio_value)


def outbound(block, shard_count, tensor_count):
    stacks, row_block, col_block = block.shape
    groups = shard_count // tensor_count
    col_flat = col_block // shard_count
    turned = jnp.swapaxes(block, 1, 2)
    return turned.reshape(stacks, groups, tensor_count, col_flat * row_block)


def arrived_flat(piece, row_block):
    stacks, shard_count, single, length = piece.shape
    col_flat = length // row_block
    spread = piece.reshape(stacks, shard_count, col_flat, row_block)
    return jnp.transpose(spread, (0, 2, 1, 3)).reshape(stacks, col_flat, shard_count * row_block)


def homebound(flat, row_block):
    stacks, col_flat, rows_all = flat.shape
    shard_count = rows_all // row_block
    spread = flat.reshape(stacks, col_flat, shard_count, row_block)
    return jnp.transpose(spread, (0, 2, 1, 3)).reshape(stacks, shard_count, 1, col_flat * row_block)


def arrived_block(piece, row_block):
    stacks, groups, tensor_count, length = piece.shape
    col_flat = length // row_block
    spread = piece.reshape(stacks, groups * tensor_count * col_flat, row_block)
    return jnp.swapaxes(spread, 1, 2)


ORDER = ((1, 0), (1, 1), (2, 0), (0, 0), (0, 1), (0, 2), (0, 3))


def row_of(array, index):
    return (0, 4, 6)[array] + index


def exchange_kernel(shard_count, tensor_count, *refs):
    weights, grads, firsts, seconds = refs[0:3], refs[3:6], refs[6:9], refs[9:12]
    updates, firsts_new, seconds_new, sums_out = refs[12:15], refs[15:18], refs[18:21], refs[21]
    grad_v, turned_v, flat_v, back_v = refs[22:25], refs[25:28], refs[28:31], refs[31:34]
    first_v, second_v, weight_v = refs[34:37], refs[37:40], refs[40:43]
    out_stop, back_stop = refs[43:46], refs[46:49]
    partial, sums_v = refs[49], refs[50]
    (
        load_g, load_m, load_v, load_w, out_send, out_recv, stop_recv, stop_send,
        back_send, back_recv, bstop_recv, bstop_send, save_u, save_m, save_v, total_sem,
    ) = refs[51:67]

    groups = shard_count // tensor_count
    half = tensor_count // 2
    devices = shard_count * tensor_count
    s, t = lax.axis_index("shard"), lax.axis_index("tensor")
    me = s * tensor_count + t
    mate = lax.rem(t + half, tensor_count)
    side = t // half
    home = s // groups
    mine = lax.rem(s, groups) * tensor_count + t
    my_slot = lax.rem(s, groups) * half + lax.rem(t, half)
    same_side = home // half == side

    for position, (a, i) in enumerate(ORDER):
        pltpu.make_async_copy(grads[a].at[i], grad_v[a].at[i], load_g.at[position]).start()
    for position, (a, i) in enumerate(ORDER):
        pltpu.make_async_copy(firsts[a].at[i], first_v[a].at[i], load_m.at[position]).start()
        pltpu.make_async_copy(seconds[a].at[i], second_v[a].at[i], load_v.at[position]).start()
        pltpu.make_async_copy(weights[a].at[i], weight_v[a].at[i], load_w.at[position]).start()

    barrier = pltpu.get_barrier_semaphore()

    def greet(step, carry):
        other = lax.rem(me + step, devices)
        pl.semaphore_signal(
            barrier,
            inc=1,
            device_id=(other // tensor_count, lax.rem(other, tensor_count)),
            device_id_type=MESH,
        )
        return carry

    lax.fori_loop(1, devices, greet, 0)

    def sizes(a):
        row_block, col_block = weights[a].shape[1:]
        return row_block, col_block, col_block // shard_count

    def remote(src, dst, send, recv, device):
        return pltpu.make_async_remote_copy(
            src_ref=src, dst_ref=dst, send_sem=send, recv_sem=recv,
            device_id=device, device_id_type=MESH,
        )

    def send_or_keep(is_me, src, dst, send, recv, device):
        @pl.when(is_me)
        def _():
            pltpu.make_async_copy(src, dst, recv).start()

        @pl.when(jnp.logical_not(is_me))
        def _():
            remote(src, dst, send, recv, device).start()

    def wait_bytes(ref, sem):
        pltpu.make_async_copy(ref, ref, sem).wait()

    def turn(position):
        a, i = ORDER[position]
        row_block, col_block, col_flat = sizes(a)
        wait_bytes(grad_v[a].at[i], load_g.at[position])

        def one(j, carry):
            span = pl.ds(pl.multiple_of(j * 128, 128), 128)
            turned_v[a][i, span, :] = grad_v[a][i, :, span].T
            return carry

        lax.fori_loop(0, col_block // 128, one, 0)

    def send_out(position):
        a, i = ORDER[position]
        row_block, col_block, col_flat = sizes(a)
        land = pl.ds(pl.multiple_of(s * row_block, 128), row_block)
        send, recv = out_send.at[position], out_recv.at[position]
        if RELAY_OUT:
            other_side = mate // half
            for y in range(groups):
                rows = pl.ds(
                    pl.multiple_of((y * tensor_count + other_side * half) * col_flat, 8),
                    half * col_flat,
                )
                remote(
                    turned_v[a].at[i, rows, :],
                    out_stop[a].at[i, pl.ds(y * half * col_flat, half * col_flat), :],
                    send,
                    stop_recv.at[position],
                    (s, mate),
                ).start()
            for y in range(groups):
                for core in range(half):
                    target = side * half + core
                    k = y * tensor_count + target
                    rows = pl.ds(pl.multiple_of(k * col_flat, 8), col_flat)
                    shard_to = groups * t + y
                    send_or_keep(
                        jnp.logical_and(shard_to == s, target == t),
                        turned_v[a].at[i, rows, :],
                        flat_v[a].at[i, :, land],
                        send,
                        recv,
                        (shard_to, target),
                    )
        else:
            for k in range(shard_count):
                shard_to, target = groups * t + k // tensor_count, k % tensor_count
                send_or_keep(
                    jnp.logical_and(shard_to == s, target == t),
                    turned_v[a].at[i, pl.ds(k * col_flat, col_flat), :],
                    flat_v[a].at[i, :, land],
                    send,
                    recv,
                    (shard_to, target),
                )

    def forward_out(position):
        if not RELAY_OUT:
            return
        a, i = ORDER[position]
        row_block, col_block, col_flat = sizes(a)
        wait_bytes(out_stop[a].at[i], stop_recv.at[position])
        land = pl.ds(pl.multiple_of(s * row_block, 128), row_block)
        for y in range(groups):
            for core in range(half):
                target = side * half + core
                shard_to = groups * mate + y
                send_or_keep(
                    jnp.logical_and(shard_to == s, target == t),
                    out_stop[a].at[i, pl.ds((y * half + core) * col_flat, col_flat), :],
                    flat_v[a].at[i, :, land],
                    stop_send.at[position],
                    out_recv.at[position],
                    (shard_to, target),
                )

    def moments(position):
        a, i = ORDER[position]
        row_block, col_block, col_flat = sizes(a)
        wait_bytes(flat_v[a].at[i], out_recv.at[position])
        wait_bytes(first_v[a].at[i], load_m.at[position])
        wait_bytes(second_v[a].at[i], load_v.at[position])
        length = shard_count * row_block
        width = 1024 if length % 1024 == 0 else row_block

        def one(j, carry):
            rows = pl.ds(pl.multiple_of(j * 8, 8), 8)
            for at in range(0, length, width):
                cols = pl.ds(at, width)
                first_new, second_new, ratio = moment_step(
                    flat_v[a][i, rows, cols], first_v[a][i, rows, cols], second_v[a][i, rows, cols]
                )
                first_v[a][i, rows, cols] = first_new
                second_v[a][i, rows, cols] = second_new
                flat_v[a][i, rows, cols] = ratio
            return carry

        lax.fori_loop(0, col_flat // 8, one, 0)
        rows = pl.ds(pl.multiple_of(mine * col_flat, 8), col_flat)
        slot = pl.ds(pl.multiple_of(my_slot * col_flat, 8), col_flat)
        for shard_to in range(shard_count):
            piece = flat_v[a].at[i, :, pl.ds(shard_to * row_block, row_block)]

            def direct():
                send_or_keep(
                    jnp.logical_and(s == shard_to, home == t),
                    piece,
                    back_v[a].at[i, rows, :],
                    back_send.at[position],
                    back_recv.at[position],
                    (shard_to, home),
                )

            def by_stop():
                stop = lax.rem(home + half, tensor_count)
                send_or_keep(
                    jnp.logical_and(s == shard_to, stop == t),
                    piece,
                    back_stop[a].at[i, slot, :],
                    back_send.at[position],
                    bstop_recv.at[position],
                    (shard_to, stop),
                )

            if RELAY_BACK:
                pl.when(same_side)(direct)
                pl.when(jnp.logical_not(same_side))(by_stop)
            else:
                direct()
        pltpu.make_async_copy(first_v[a].at[i], firsts_new[a].at[i], save_m.at[position]).start()
        pltpu.make_async_copy(second_v[a].at[i], seconds_new[a].at[i], save_v.at[position]).start()

    def forward_back(position):
        if not RELAY_BACK:
            return
        a, i = ORDER[position]
        row_block, col_block, col_flat = sizes(a)
        wait_bytes(back_stop[a].at[i], bstop_recv.at[position])
        for y in range(groups):
            rows = pl.ds(
                pl.multiple_of((y * tensor_count + side * half) * col_flat, 8), half * col_flat
            )
            remote(
                back_stop[a].at[i, pl.ds(y * half * col_flat, half * col_flat), :],
                back_v[a].at[i, rows, :],
                bstop_send.at[position],
                back_recv.at[position],
                (s, mate),
            ).start()

    def renew(position):
        a, i = ORDER[position]
        row_block, col_block, col_flat = sizes(a)
        wait_bytes(back_v[a].at[i], back_recv.at[position])
        wait_bytes(weight_v[a].at[i], load_w.at[position])

        def fold(block):
            return jnp.sum((block * block).reshape(row_block // 8, 8, 128), axis=0)

        def one(j, carry):
            span = pl.ds(pl.multiple_of(j * 128, 128), 128)
            weight = weight_v[a][i, :, span]
            update = back_v[a][i, span, :].T + decay_rate * weight
            grad_v[a][i, :, span] = update
            return carry[0] + fold(weight), carry[1] + fold(update)

        zero = jnp.zeros((8, 128), jnp.float32)
        weight_sq, update_sq = lax.fori_loop(0, col_block // 128, one, (zero, zero))
        row = row_of(a, i)
        partial[me, row : row + 1, :] = jnp.sum(weight_sq, axis=0, keepdims=True)
        partial[me, row + 8 : row + 9, :] = jnp.sum(update_sq, axis=0, keepdims=True)
        pltpu.make_async_copy(grad_v[a].at[i], updates[a].at[i], save_u.at[position]).start()

    count = len(ORDER)
    partial[me, :, :] = jnp.zeros((16, 128), jnp.float32)
    turn(0)
    pl.semaphore_wait(barrier, devices - 1)
    send_out(0)
    for position in range(1, count):
        turn(position)
        send_out(position)
    forward_out(0)
    for position in range(count):
        if position + 1 < count:
            forward_out(position + 1)
        moments(position)
        if position >= 2:
            forward_back(position - 2)
    renew(0)
    forward_back(count - 2)
    renew(1)
    forward_back(count - 1)
    for position in range(2, count):
        renew(position)

    def tell(step, carry):
        other = lax.rem(me + step, devices)
        remote(
            partial.at[me],
            partial.at[me],
            total_sem.at[0],
            total_sem.at[1],
            (other // tensor_count, lax.rem(other, tensor_count)),
        ).start()
        return carry

    lax.fori_loop(1, devices, tell, 0)
    wait_bytes(partial.at[pl.ds(0, devices - 1)], total_sem.at[1])
    total = lax.fori_loop(
        0, devices, lambda d, sofar: sofar + partial[d], jnp.zeros((16, 128), jnp.float32)
    )
    sums_v[...] = total
    pltpu.make_async_copy(sums_v, sums_out, total_sem.at[2]).start()
    wait_bytes(partial.at[pl.ds(0, devices - 1)], total_sem.at[0])

    out_self = home == t if RELAY_OUT else home == t
    stop_self = home == mate
    back_self = home == t
    if RELAY_BACK:
        back_self = jnp.logical_or(home == t, lax.rem(home + half, tensor_count) == t)

    def wait_less(is_less, ref, i, total_rows, piece_rows, sem):
        @pl.when(is_less)
        def _():
            wait_bytes(ref.at[i, pl.ds(0, total_rows - piece_rows), :], sem)

        @pl.when(jnp.logical_not(is_less))
        def _():
            wait_bytes(ref.at[i], sem)

    for position, (a, i) in enumerate(ORDER):
        row_block, col_block, col_flat = sizes(a)
        wait_less(out_self, turned_v[a], i, col_block, col_flat, out_send.at[position])
        wait_less(back_self, turned_v[a], i, col_block, col_flat, back_send.at[position])
        if RELAY_OUT:
            wait_less(stop_self, out_stop[a], i, col_block // 2, col_flat, stop_send.at[position])
        if RELAY_BACK:
            wait_bytes(back_stop[a].at[i], bstop_send.at[position])
        wait_bytes(grad_v[a].at[i], save_u.at[position])
        wait_bytes(first_v[a].at[i], save_m.at[position])
        wait_bytes(second_v[a].at[i], save_v.at[position])
    wait_bytes(sums_v, total_sem.at[2])


def exchange(weights, grads, firsts, seconds, shard_count, tensor_count):
    f32 = jnp.float32
    blocks = [matrix.shape for matrix in weights]
    flats = [matrix.shape for matrix in firsts]
    turned = [(n, c, r) for n, r, c in blocks]
    halves = [(n, c // 2, r) for n, r, c in blocks]
    devices = shard_count * tensor_count
    shapes = blocks + flats + flats + [(16, 128)]
    scratch = []
    for group in (blocks, turned, flats, turned, flats, flats, blocks, halves, halves):
        scratch += [pltpu.VMEM(shape, f32) for shape in group]
    scratch += [pltpu.VMEM((devices, 16, 128), f32), pltpu.VMEM((16, 128), f32)]
    scratch += [pltpu.SemaphoreType.DMA((len(ORDER),))] * 15 + [pltpu.SemaphoreType.DMA((3,))]
    anywhere = pl.BlockSpec(memory_space=pl.ANY)
    return pl.pallas_call(
        functools.partial(exchange_kernel, shard_count, tensor_count),
        out_shape=[jax.ShapeDtypeStruct(shape, f32) for shape in shapes],
        in_specs=[anywhere] * 12,
        out_specs=[anywhere] * 10,
        scratch_shapes=scratch,
        compiler_params=pltpu.CompilerParams(
            collective_id=0, has_side_effects=True, vmem_limit_bytes=56 * 1024 * 1024
        ),
        name="exchange",
    )(*weights, *grads, *firsts, *seconds)


def fits(weights, firsts, shard_count, tensor_count):
    if shard_count % tensor_count or tensor_count % 2:
        return False
    return all(
        matrix.shape[1] % 128 == 0
        and matrix.shape[2] % 128 == 0
        and matrix.shape[2] % (8 * shard_count) == 0
        for matrix in weights
    )


def shards(*arrays):
    shard_count = lax.axis_size("shard")
    tensor_count = lax.axis_size("tensor")
    weights, grads, firsts, seconds = arrays[0:3], arrays[3:6], arrays[6:9], arrays[9:12]
    if not fits(weights, firsts, shard_count, tensor_count):
        return plain(weights, grads, firsts, seconds, shard_count, tensor_count)
    out = exchange(weights, grads, firsts, seconds, shard_count, tensor_count)
    updates, firsts_new, seconds_new, sums = out[0:3], out[3:6], out[6:9], out[9]
    totals = jnp.sum(sums, axis=1)
    trust_ratio = jnp.sqrt(totals[0:7]) / (jnp.sqrt(totals[8:15]) + epsilon)
    return finish(weights, updates, firsts_new, seconds_new, trust_ratio)


def finish(weights, updates, firsts_new, seconds_new, trust_ratio):
    scales = (trust_ratio[0:4], trust_ratio[4:6], trust_ratio[6:7])
    new_weights = [
        weights[position] - learn_rate * scales[position][:, None, None] * updates[position]
        for position in range(3)
    ]
    return (*new_weights, *firsts_new, *seconds_new, trust_ratio)


def plain(weights, grads, firsts, seconds, shard_count, tensor_count):
    row_blocks = [matrix.shape[1] for matrix in weights]
    results = []
    updates = []
    for position in range(3):
        piece = lax.all_to_all(
            lax.all_to_all(
                outbound(grads[position], shard_count, tensor_count),
                "tensor", split_axis=2, concat_axis=1, tiled=True,
            ),
            "shard", split_axis=1, concat_axis=1, tiled=True,
        )
        flat = arrived_flat(piece, row_blocks[position])
        results.append(moment_step(flat, firsts[position], seconds[position]))
        restored = lax.all_to_all(
            lax.all_to_all(
                homebound(results[position][2], row_blocks[position]),
                "shard", split_axis=1, concat_axis=1, tiled=True,
            ),
            "tensor", split_axis=1, concat_axis=2, tiled=True,
        )
        ratio = arrived_block(restored, row_blocks[position])
        updates.append(ratio + decay_rate * weights[position])
    weight_sq = jnp.concatenate([jnp.sum(member * member, axis=(1, 2)) for member in weights])
    update_sq = jnp.concatenate([jnp.sum(member * member, axis=(1, 2)) for member in updates])
    weight_total, update_total = lax.psum((weight_sq, update_sq), ("shard", "tensor"))
    trust_ratio = jnp.sqrt(weight_total) / (jnp.sqrt(update_total) + epsilon)
    return finish(
        weights, updates, [r[0] for r in results], [r[1] for r in results], trust_ratio
    )


def solution(mesh):
    in_specs = (
        P(None, "shard", "tensor"),
        P(None, "shard", "tensor"),
        P(None, "shard", "tensor"),
        P(None, "shard", "tensor"),
        P(None, "shard", "tensor"),
        P(None, "shard", "tensor"),
        P(None, ("shard", "tensor"), None),
        P(None, ("shard", "tensor"), None),
        P(None, ("shard", "tensor"), None),
        P(None, ("shard", "tensor"), None),
        P(None, ("shard", "tensor"), None),
        P(None, ("shard", "tensor"), None),
    )
    out_specs = (
        P(None, "shard", "tensor"),
        P(None, "shard", "tensor"),
        P(None, "shard", "tensor"),
        P(None, ("shard", "tensor"), None),
        P(None, ("shard", "tensor"), None),
        P(None, ("shard", "tensor"), None),
        P(None, ("shard", "tensor"), None),
        P(None, ("shard", "tensor"), None),
        P(None, ("shard", "tensor"), None),
        P(),
    )
    return jax.shard_map(shards, mesh=mesh, in_specs=in_specs, out_specs=out_specs, check_vma=False)
```

```python
import functools

import jax
import jax.numpy as jnp
from jax import lax
from jax.experimental import pallas as pl
from jax.experimental.pallas import tpu as pltpu
from jax.sharding import PartitionSpec as P

MESH = pl.DeviceIdType.MESH
RELAY_OUT = True
RELAY_BACK = True

beta_one = 0.9
beta_two = 0.999
step_number = 10.0
correct_one = 1.0 - beta_one**step_number
correct_two = 1.0 - beta_two**step_number
learn_rate = 0.02
decay_rate = 0.1
epsilon = 1e-06


def moment_step(gradient_t, first_moment, second):
    first_new = beta_one * first_moment + (1.0 - beta_one) * gradient_t
    second_new = beta_two * second + (1.0 - beta_two) * gradient_t * gradient_t
    ratio_value = first_new / correct_one / (jnp.sqrt(second_new / correct_two) + epsilon)
    return (first_new, second_new, ratio_value)


def outbound(block, shard_count, tensor_count):
    stacks, row_block, col_block = block.shape
    groups = shard_count // tensor_count
    col_flat = col_block // shard_count
    turned = jnp.swapaxes(block, 1, 2)
    return turned.reshape(stacks, groups, tensor_count, col_flat * row_block)


def arrived_flat(piece, row_block):
    stacks, shard_count, single, length = piece.shape
    col_flat = length // row_block
    spread = piece.reshape(stacks, shard_count, col_flat, row_block)
    return jnp.transpose(spread, (0, 2, 1, 3)).reshape(stacks, col_flat, shard_count * row_block)


def homebound(flat, row_block):
    stacks, col_flat, rows_all = flat.shape
    shard_count = rows_all // row_block
    spread = flat.reshape(stacks, col_flat, shard_count, row_block)
    return jnp.transpose(spread, (0, 2, 1, 3)).reshape(stacks, shard_count, 1, col_flat * row_block)


def arrived_block(piece, row_block):
    stacks, groups, tensor_count, length = piece.shape
    col_flat = length // row_block
    spread = piece.reshape(stacks, groups * tensor_count * col_flat, row_block)
    return jnp.swapaxes(spread, 1, 2)


ORDER = ((1, 0), (1, 1), (2, 0), (0, 0), (0, 1), (0, 2), (0, 3))


def row_of(array, index):
    return (0, 4, 6)[array] + index


def exchange_kernel(shard_count, tensor_count, *refs):
    weights, grads, firsts, seconds = refs[0:3], refs[3:6], refs[6:9], refs[9:12]
    updates, firsts_new, seconds_new, sums_out = refs[12:15], refs[15:18], refs[18:21], refs[21]
    grad_v, turned_v, flat_v, back_v = refs[22:25], refs[25:28], refs[28:31], refs[31:34]
    first_v, second_v, weight_v = refs[34:37], refs[37:40], refs[40:43]
    out_stop, back_stop = refs[43:46], refs[46:49]
    partial, sums_v = refs[49], refs[50]
    (
        load_g, load_m, load_v, load_w, out_send, out_recv, stop_recv, stop_send,
        back_send, back_recv, bstop_recv, bstop_send, save_u, save_m, save_v, total_sem,
    ) = refs[51:67]

    groups = shard_count // tensor_count
    half = tensor_count // 2
    devices = shard_count * tensor_count
    s, t = lax.axis_index("shard"), lax.axis_index("tensor")
    me = s * tensor_count + t
    mate = lax.rem(t + half, tensor_count)
    side = t // half
    home = s // groups
    mine = lax.rem(s, groups) * tensor_count + t
    my_slot = lax.rem(s, groups) * half + lax.rem(t, half)
    same_side = home // half == side

    for position, (a, i) in enumerate(ORDER):
        pltpu.make_async_copy(grads[a].at[i], grad_v[a].at[i], load_g.at[position]).start()
    for position, (a, i) in enumerate(ORDER):
        pltpu.make_async_copy(firsts[a].at[i], first_v[a].at[i], load_m.at[position]).start()
        pltpu.make_async_copy(seconds[a].at[i], second_v[a].at[i], load_v.at[position]).start()
        pltpu.make_async_copy(weights[a].at[i], weight_v[a].at[i], load_w.at[position]).start()

    barrier = pltpu.get_barrier_semaphore()

    def greet(step, carry):
        other = lax.rem(me + step, devices)
        pl.semaphore_signal(
            barrier,
            inc=1,
            device_id=(other // tensor_count, lax.rem(other, tensor_count)),
            device_id_type=MESH,
        )
        return carry

    lax.fori_loop(1, devices, greet, 0)

    def sizes(a):
        row_block, col_block = weights[a].shape[1:]
        return row_block, col_block, col_block // shard_count

    def remote(src, dst, send, recv, device):
        return pltpu.make_async_remote_copy(
            src_ref=src, dst_ref=dst, send_sem=send, recv_sem=recv,
            device_id=device, device_id_type=MESH,
        )

    def send_or_keep(is_me, src, dst, send, recv, device):
        @pl.when(is_me)
        def _():
            pltpu.make_async_copy(src, dst, recv).start()

        @pl.when(jnp.logical_not(is_me))
        def _():
            remote(src, dst, send, recv, device).start()

    def wait_bytes(ref, sem):
        pltpu.make_async_copy(ref, ref, sem).wait()

    def turn(position):
        a, i = ORDER[position]
        row_block, col_block, col_flat = sizes(a)
        wait_bytes(grad_v[a].at[i], load_g.at[position])

        def one(j, carry):
            span = pl.ds(pl.multiple_of(j * 128, 128), 128)
            turned_v[a][i, span, :] = grad_v[a][i, :, span].T
            return carry

        lax.fori_loop(0, col_block // 128, one, 0)

    def send_out(position):
        a, i = ORDER[position]
        row_block, col_block, col_flat = sizes(a)
        land = pl.ds(pl.multiple_of(s * row_block, 128), row_block)
        send, recv = out_send.at[position], out_recv.at[position]
        if RELAY_OUT:
            other_side = mate // half
            for y in range(groups):
                rows = pl.ds(
                    pl.multiple_of((y * tensor_count + other_side * half) * col_flat, 8),
                    half * col_flat,
                )
                remote(
                    turned_v[a].at[i, rows, :],
                    out_stop[a].at[i, pl.ds(y * half * col_flat, half * col_flat), :],
                    send,
                    stop_recv.at[position],
                    (s, mate),
                ).start()
            for y in range(groups):
                for core in range(half):
                    target = side * half + core
                    k = y * tensor_count + target
                    rows = pl.ds(pl.multiple_of(k * col_flat, 8), col_flat)
                    shard_to = groups * t + y
                    send_or_keep(
                        jnp.logical_and(shard_to == s, target == t),
                        turned_v[a].at[i, rows, :],
                        flat_v[a].at[i, :, land],
                        send,
                        recv,
                        (shard_to, target),
                    )
        else:
            for k in range(shard_count):
                shard_to, target = groups * t + k // tensor_count, k % tensor_count
                send_or_keep(
                    jnp.logical_and(shard_to == s, target == t),
                    turned_v[a].at[i, pl.ds(k * col_flat, col_flat), :],
                    flat_v[a].at[i, :, land],
                    send,
                    recv,
                    (shard_to, target),
                )

    def forward_out(position):
        if not RELAY_OUT:
            return
        a, i = ORDER[position]
        row_block, col_block, col_flat = sizes(a)
        wait_bytes(out_stop[a].at[i], stop_recv.at[position])
        land = pl.ds(pl.multiple_of(s * row_block, 128), row_block)
        for y in range(groups):
            for core in range(half):
                target = side * half + core
                shard_to = groups * mate + y
                send_or_keep(
                    jnp.logical_and(shard_to == s, target == t),
                    out_stop[a].at[i, pl.ds((y * half + core) * col_flat, col_flat), :],
                    flat_v[a].at[i, :, land],
                    stop_send.at[position],
                    out_recv.at[position],
                    (shard_to, target),
                )

    def moments(position):
        a, i = ORDER[position]
        row_block, col_block, col_flat = sizes(a)
        wait_bytes(flat_v[a].at[i], out_recv.at[position])
        wait_bytes(first_v[a].at[i], load_m.at[position])
        wait_bytes(second_v[a].at[i], load_v.at[position])
        length = shard_count * row_block
        width = 1024 if length % 1024 == 0 else row_block

        def one(j, carry):
            rows = pl.ds(pl.multiple_of(j * 8, 8), 8)
            for at in range(0, length, width):
                cols = pl.ds(at, width)
                first_new, second_new, ratio = moment_step(
                    flat_v[a][i, rows, cols], first_v[a][i, rows, cols], second_v[a][i, rows, cols]
                )
                first_v[a][i, rows, cols] = first_new
                second_v[a][i, rows, cols] = second_new
                flat_v[a][i, rows, cols] = ratio
            return carry

        lax.fori_loop(0, col_flat // 8, one, 0)
        rows = pl.ds(pl.multiple_of(mine * col_flat, 8), col_flat)
        slot = pl.ds(pl.multiple_of(my_slot * col_flat, 8), col_flat)
        for shard_to in range(shard_count):
            piece = flat_v[a].at[i, :, pl.ds(shard_to * row_block, row_block)]

            def direct():
                send_or_keep(
                    jnp.logical_and(s == shard_to, home == t),
                    piece,
                    back_v[a].at[i, rows, :],
                    back_send.at[position],
                    back_recv.at[position],
                    (shard_to, home),
                )

            def by_stop():
                stop = lax.rem(home + half, tensor_count)
                send_or_keep(
                    jnp.logical_and(s == shard_to, stop == t),
                    piece,
                    back_stop[a].at[i, slot, :],
                    back_send.at[position],
                    bstop_recv.at[position],
                    (shard_to, stop),
                )

            if RELAY_BACK:
                pl.when(same_side)(direct)
                pl.when(jnp.logical_not(same_side))(by_stop)
            else:
                direct()
        pltpu.make_async_copy(first_v[a].at[i], firsts_new[a].at[i], save_m.at[position]).start()
        pltpu.make_async_copy(second_v[a].at[i], seconds_new[a].at[i], save_v.at[position]).start()

    def forward_back(position):
        if not RELAY_BACK:
            return
        a, i = ORDER[position]
        row_block, col_block, col_flat = sizes(a)
        wait_bytes(back_stop[a].at[i], bstop_recv.at[position])
        for y in range(groups):
            rows = pl.ds(
                pl.multiple_of((y * tensor_count + side * half) * col_flat, 8), half * col_flat
            )
            remote(
                back_stop[a].at[i, pl.ds(y * half * col_flat, half * col_flat), :],
                back_v[a].at[i, rows, :],
                bstop_send.at[position],
                back_recv.at[position],
                (s, mate),
            ).start()

    def renew(position):
        a, i = ORDER[position]
        row_block, col_block, col_flat = sizes(a)
        wait_bytes(back_v[a].at[i], back_recv.at[position])
        wait_bytes(weight_v[a].at[i], load_w.at[position])

        def fold(block):
            return jnp.sum((block * block).reshape(row_block // 8, 8, 128), axis=0)

        def one(j, carry):
            span = pl.ds(pl.multiple_of(j * 128, 128), 128)
            weight = weight_v[a][i, :, span]
            update = back_v[a][i, span, :].T + decay_rate * weight
            grad_v[a][i, :, span] = update
            return carry[0] + fold(weight), carry[1] + fold(update)

        zero = jnp.zeros((8, 128), jnp.float32)
        weight_sq, update_sq = lax.fori_loop(0, col_block // 128, one, (zero, zero))
        row = row_of(a, i)
        partial[me, row : row + 1, :] = jnp.sum(weight_sq, axis=0, keepdims=True)
        partial[me, row + 8 : row + 9, :] = jnp.sum(update_sq, axis=0, keepdims=True)
        pltpu.make_async_copy(grad_v[a].at[i], updates[a].at[i], save_u.at[position]).start()

    count = len(ORDER)
    partial[me, :, :] = jnp.zeros((16, 128), jnp.float32)
    turn(0)
    pl.semaphore_wait(barrier, devices - 1)
    send_out(0)
    for position in range(1, count):
        turn(position)
        send_out(position)
    forward_out(0)
    for position in range(count):
        if position + 1 < count:
            forward_out(position + 1)
        moments(position)
        if position >= 2:
            forward_back(position - 2)
    renew(0)
    forward_back(count - 2)
    renew(1)
    forward_back(count - 1)
    for position in range(2, count):
        renew(position)

    def tell(step, carry):
        other = lax.rem(me + step, devices)
        remote(
            partial.at[me],
            partial.at[me],
            total_sem.at[0],
            total_sem.at[1],
            (other // tensor_count, lax.rem(other, tensor_count)),
        ).start()
        return carry

    lax.fori_loop(1, devices, tell, 0)
    wait_bytes(partial.at[pl.ds(0, devices - 1)], total_sem.at[1])
    total = lax.fori_loop(
        0, devices, lambda d, sofar: sofar + partial[d], jnp.zeros((16, 128), jnp.float32)
    )
    sums_v[...] = total
    pltpu.make_async_copy(sums_v, sums_out, total_sem.at[2]).start()
    wait_bytes(partial.at[pl.ds(0, devices - 1)], total_sem.at[0])

    out_self = home == t if RELAY_OUT else home == t
    stop_self = home == mate
    back_self = home == t
    if RELAY_BACK:
        back_self = jnp.logical_or(home == t, lax.rem(home + half, tensor_count) == t)

    def wait_less(is_less, ref, i, total_rows, piece_rows, sem):
        @pl.when(is_less)
        def _():
            wait_bytes(ref.at[i, pl.ds(0, total_rows - piece_rows), :], sem)

        @pl.when(jnp.logical_not(is_less))
        def _():
            wait_bytes(ref.at[i], sem)

    for position, (a, i) in enumerate(ORDER):
        row_block, col_block, col_flat = sizes(a)
        wait_less(out_self, turned_v[a], i, col_block, col_flat, out_send.at[position])
        wait_less(back_self, turned_v[a], i, col_block, col_flat, back_send.at[position])
        if RELAY_OUT:
            wait_less(stop_self, out_stop[a], i, col_block // 2, col_flat, stop_send.at[position])
        if RELAY_BACK:
            wait_bytes(back_stop[a].at[i], bstop_send.at[position])
        wait_bytes(grad_v[a].at[i], save_u.at[position])
        wait_bytes(first_v[a].at[i], save_m.at[position])
        wait_bytes(second_v[a].at[i], save_v.at[position])
    wait_bytes(sums_v, total_sem.at[2])


def exchange(weights, grads, firsts, seconds, shard_count, tensor_count):
    f32 = jnp.float32
    blocks = [matrix.shape for matrix in weights]
    flats = [matrix.shape for matrix in firsts]
    turned = [(n, c, r) for n, r, c in blocks]
    halves = [(n, c // 2, r) for n, r, c in blocks]
    devices = shard_count * tensor_count
    shapes = blocks + flats + flats + [(16, 128)]
    scratch = []
    for group in (blocks, turned, flats, turned, flats, flats, blocks, halves, halves):
        scratch += [pltpu.VMEM(shape, f32) for shape in group]
    scratch += [pltpu.VMEM((devices, 16, 128), f32), pltpu.VMEM((16, 128), f32)]
    scratch += [pltpu.SemaphoreType.DMA((len(ORDER),))] * 15 + [pltpu.SemaphoreType.DMA((3,))]
    anywhere = pl.BlockSpec(memory_space=pl.ANY)
    return pl.pallas_call(
        functools.partial(exchange_kernel, shard_count, tensor_count),
        out_shape=[jax.ShapeDtypeStruct(shape, f32) for shape in shapes],
        in_specs=[anywhere] * 12,
        out_specs=[anywhere] * 10,
        scratch_shapes=scratch,
        compiler_params=pltpu.CompilerParams(
            collective_id=0, has_side_effects=True, vmem_limit_bytes=56 * 1024 * 1024
        ),
        name="exchange",
    )(*weights, *grads, *firsts, *seconds)


def fits(weights, firsts, shard_count, tensor_count):
    if shard_count % tensor_count or tensor_count % 2:
        return False
    return all(
        matrix.shape[1] % 128 == 0
        and matrix.shape[2] % 128 == 0
        and matrix.shape[2] % (8 * shard_count) == 0
        for matrix in weights
    )


def shards(*arrays):
    shard_count = lax.axis_size("shard")
    tensor_count = lax.axis_size("tensor")
    weights, grads, firsts, seconds = arrays[0:3], arrays[3:6], arrays[6:9], arrays[9:12]
    if not fits(weights, firsts, shard_count, tensor_count):
        return plain(weights, grads, firsts, seconds, shard_count, tensor_count)
    out = exchange(weights, grads, firsts, seconds, shard_count, tensor_count)
    updates, firsts_new, seconds_new, sums = out[0:3], out[3:6], out[6:9], out[9]
    totals = jnp.sum(sums, axis=1)
    trust_ratio = jnp.sqrt(totals[0:7]) / (jnp.sqrt(totals[8:15]) + epsilon)
    return finish(weights, updates, firsts_new, seconds_new, trust_ratio)


def finish(weights, updates, firsts_new, seconds_new, trust_ratio):
    scales = (trust_ratio[0:4], trust_ratio[4:6], trust_ratio[6:7])
    new_weights = [
        weights[position] - learn_rate * scales[position][:, None, None] * updates[position]
        for position in range(3)
    ]
    return (*new_weights, *firsts_new, *seconds_new, trust_ratio)


def plain(weights, grads, firsts, seconds, shard_count, tensor_count):
    row_blocks = [matrix.shape[1] for matrix in weights]
    results = []
    updates = []
    for position in range(3):
        piece = lax.all_to_all(
            lax.all_to_all(
                outbound(grads[position], shard_count, tensor_count),
                "tensor", split_axis=2, concat_axis=1, tiled=True,
            ),
            "shard", split_axis=1, concat_axis=1, tiled=True,
        )
        flat = arrived_flat(piece, row_blocks[position])
        results.append(moment_step(flat, firsts[position], seconds[position]))
        restored = lax.all_to_all(
            lax.all_to_all(
                homebound(results[position][2], row_blocks[position]),
                "shard", split_axis=1, concat_axis=1, tiled=True,
            ),
            "tensor", split_axis=1, concat_axis=2, tiled=True,
        )
        ratio = arrived_block(restored, row_blocks[position])
        updates.append(ratio + decay_rate * weights[position])
    weight_sq = jnp.concatenate([jnp.sum(member * member, axis=(1, 2)) for member in weights])
    update_sq = jnp.concatenate([jnp.sum(member * member, axis=(1, 2)) for member in updates])
    weight_total, update_total = lax.psum((weight_sq, update_sq), ("shard", "tensor"))
    trust_ratio = jnp.sqrt(weight_total) / (jnp.sqrt(update_total) + epsilon)
    return finish(
        weights, updates, [r[0] for r in results], [r[1] for r in results], trust_ratio
    )


def solution(mesh):
    in_specs = (
        P(None, "shard", "tensor"),
        P(None, "shard", "tensor"),
        P(None, "shard", "tensor"),
        P(None, "shard", "tensor"),
        P(None, "shard", "tensor"),
        P(None, "shard", "tensor"),
        P(None, ("shard", "tensor"), None),
        P(None, ("shard", "tensor"), None),
        P(None, ("shard", "tensor"), None),
        P(None, ("shard", "tensor"), None),
        P(None, ("shard", "tensor"), None),
        P(None, ("shard", "tensor"), None),
    )
    out_specs = (
        P(None, "shard", "tensor"),
        P(None, "shard", "tensor"),
        P(None, "shard", "tensor"),
        P(None, ("shard", "tensor"), None),
        P(None, ("shard", "tensor"), None),
        P(None, ("shard", "tensor"), None),
        P(None, ("shard", "tensor"), None),
        P(None, ("shard", "tensor"), None),
        P(None, ("shard", "tensor"), None),
        P(),
    )
    return jax.shard_map(shards, mesh=mesh, in_specs=in_specs, out_specs=out_specs, check_vma=False)
```

```python
import functools

import jax
import jax.numpy as jnp
from jax import lax
from jax.experimental import pallas as pl
from jax.experimental.pallas import tpu as pltpu
from jax.sharding import PartitionSpec as P

MESH = pl.DeviceIdType.MESH
RELAY_OUT = False
RELAY_BACK = True

beta_one = 0.9
beta_two = 0.999
step_number = 10.0
correct_one = 1.0 - beta_one**step_number
correct_two = 1.0 - beta_two**step_number
learn_rate = 0.02
decay_rate = 0.1
epsilon = 1e-06


def moment_step(gradient_t, first_moment, second):
    first_new = beta_one * first_moment + (1.0 - beta_one) * gradient_t
    second_new = beta_two * second + (1.0 - beta_two) * gradient_t * gradient_t
    ratio_value = first_new / correct_one / (jnp.sqrt(second_new / correct_two) + epsilon)
    return (first_new, second_new, ratio_value)


def outbound(block, shard_count, tensor_count):
    stacks, row_block, col_block = block.shape
    groups = shard_count // tensor_count
    col_flat = col_block // shard_count
    turned = jnp.swapaxes(block, 1, 2)
    return turned.reshape(stacks, groups, tensor_count, col_flat * row_block)


def arrived_flat(piece, row_block):
    stacks, shard_count, single, length = piece.shape
    col_flat = length // row_block
    spread = piece.reshape(stacks, shard_count, col_flat, row_block)
    return jnp.transpose(spread, (0, 2, 1, 3)).reshape(stacks, col_flat, shard_count * row_block)


def homebound(flat, row_block):
    stacks, col_flat, rows_all = flat.shape
    shard_count = rows_all // row_block
    spread = flat.reshape(stacks, col_flat, shard_count, row_block)
    return jnp.transpose(spread, (0, 2, 1, 3)).reshape(stacks, shard_count, 1, col_flat * row_block)


def arrived_block(piece, row_block):
    stacks, groups, tensor_count, length = piece.shape
    col_flat = length // row_block
    spread = piece.reshape(stacks, groups * tensor_count * col_flat, row_block)
    return jnp.swapaxes(spread, 1, 2)


ORDER = ((1, 0), (1, 1), (2, 0), (0, 0), (0, 1), (0, 2), (0, 3))


def row_of(array, index):
    return (0, 4, 6)[array] + index


def exchange_kernel(shard_count, tensor_count, *refs):
    weights, grads, firsts, seconds = refs[0:3], refs[3:6], refs[6:9], refs[9:12]
    updates, firsts_new, seconds_new, sums_out = refs[12:15], refs[15:18], refs[18:21], refs[21]
    grad_v, turned_v, flat_v, back_v = refs[22:25], refs[25:28], refs[28:31], refs[31:34]
    first_v, second_v, weight_v = refs[34:37], refs[37:40], refs[40:43]
    out_stop, back_stop = refs[43:46], refs[46:49]
    partial, sums_v = refs[49], refs[50]
    (
        load_g, load_m, load_v, load_w, out_send, out_recv, stop_recv, stop_send,
        back_send, back_recv, bstop_recv, bstop_send, save_u, save_m, save_v, total_sem,
    ) = refs[51:67]

    groups = shard_count // tensor_count
    half = tensor_count // 2
    devices = shard_count * tensor_count
    s, t = lax.axis_index("shard"), lax.axis_index("tensor")
    me = s * tensor_count + t
    mate = lax.rem(t + half, tensor_count)
    side = t // half
    home = s // groups
    mine = lax.rem(s, groups) * tensor_count + t
    my_slot = lax.rem(s, groups) * half + lax.rem(t, half)
    same_side = home // half == side

    for position, (a, i) in enumerate(ORDER):
        pltpu.make_async_copy(grads[a].at[i], grad_v[a].at[i], load_g.at[position]).start()
    for position, (a, i) in enumerate(ORDER):
        pltpu.make_async_copy(firsts[a].at[i], first_v[a].at[i], load_m.at[position]).start()
        pltpu.make_async_copy(seconds[a].at[i], second_v[a].at[i], load_v.at[position]).start()
        pltpu.make_async_copy(weights[a].at[i], weight_v[a].at[i], load_w.at[position]).start()

    barrier = pltpu.get_barrier_semaphore()

    def greet(step, carry):
        other = lax.rem(me + step, devices)
        pl.semaphore_signal(
            barrier,
            inc=1,
            device_id=(other // tensor_count, lax.rem(other, tensor_count)),
            device_id_type=MESH,
        )
        return carry

    lax.fori_loop(1, devices, greet, 0)

    def sizes(a):
        row_block, col_block = weights[a].shape[1:]
        return row_block, col_block, col_block // shard_count

    def remote(src, dst, send, recv, device):
        return pltpu.make_async_remote_copy(
            src_ref=src, dst_ref=dst, send_sem=send, recv_sem=recv,
            device_id=device, device_id_type=MESH,
        )

    def send_or_keep(is_me, src, dst, send, recv, device):
        @pl.when(is_me)
        def _():
            pltpu.make_async_copy(src, dst, recv).start()

        @pl.when(jnp.logical_not(is_me))
        def _():
            remote(src, dst, send, recv, device).start()

    def wait_bytes(ref, sem):
        pltpu.make_async_copy(ref, ref, sem).wait()

    def turn(position):
        a, i = ORDER[position]
        row_block, col_block, col_flat = sizes(a)
        wait_bytes(grad_v[a].at[i], load_g.at[position])

        def one(j, carry):
            span = pl.ds(pl.multiple_of(j * 128, 128), 128)
            turned_v[a][i, span, :] = grad_v[a][i, :, span].T
            return carry

        lax.fori_loop(0, col_block // 128, one, 0)

    def send_out(position):
        a, i = ORDER[position]
        row_block, col_block, col_flat = sizes(a)
        land = pl.ds(pl.multiple_of(s * row_block, 128), row_block)
        send, recv = out_send.at[position], out_recv.at[position]
        if RELAY_OUT:
            other_side = mate // half
            for y in range(groups):
                rows = pl.ds(
                    pl.multiple_of((y * tensor_count + other_side * half) * col_flat, 8),
                    half * col_flat,
                )
                remote(
                    turned_v[a].at[i, rows, :],
                    out_stop[a].at[i, pl.ds(y * half * col_flat, half * col_flat), :],
                    send,
                    stop_recv.at[position],
                    (s, mate),
                ).start()
            for y in range(groups):
                for core in range(half):
                    target = side * half + core
                    k = y * tensor_count + target
                    rows = pl.ds(pl.multiple_of(k * col_flat, 8), col_flat)
                    shard_to = groups * t + y
                    send_or_keep(
                        jnp.logical_and(shard_to == s, target == t),
                        turned_v[a].at[i, rows, :],
                        flat_v[a].at[i, :, land],
                        send,
                        recv,
                        (shard_to, target),
                    )
        else:
            for k in range(shard_count):
                shard_to, target = groups * t + k // tensor_count, k % tensor_count
                send_or_keep(
                    jnp.logical_and(shard_to == s, target == t),
                    turned_v[a].at[i, pl.ds(k * col_flat, col_flat), :],
                    flat_v[a].at[i, :, land],
                    send,
                    recv,
                    (shard_to, target),
                )

    def forward_out(position):
        if not RELAY_OUT:
            return
        a, i = ORDER[position]
        row_block, col_block, col_flat = sizes(a)
        wait_bytes(out_stop[a].at[i], stop_recv.at[position])
        land = pl.ds(pl.multiple_of(s * row_block, 128), row_block)
        for y in range(groups):
            for core in range(half):
                target = side * half + core
                shard_to = groups * mate + y
                send_or_keep(
                    jnp.logical_and(shard_to == s, target == t),
                    out_stop[a].at[i, pl.ds((y * half + core) * col_flat, col_flat), :],
                    flat_v[a].at[i, :, land],
                    stop_send.at[position],
                    out_recv.at[position],
                    (shard_to, target),
                )

    def moments(position):
        a, i = ORDER[position]
        row_block, col_block, col_flat = sizes(a)
        wait_bytes(flat_v[a].at[i], out_recv.at[position])
        wait_bytes(first_v[a].at[i], load_m.at[position])
        wait_bytes(second_v[a].at[i], load_v.at[position])
        length = shard_count * row_block
        width = 1024 if length % 1024 == 0 else row_block

        def one(j, carry):
            rows = pl.ds(pl.multiple_of(j * 8, 8), 8)
            for at in range(0, length, width):
                cols = pl.ds(at, width)
                first_new, second_new, ratio = moment_step(
                    flat_v[a][i, rows, cols], first_v[a][i, rows, cols], second_v[a][i, rows, cols]
                )
                first_v[a][i, rows, cols] = first_new
                second_v[a][i, rows, cols] = second_new
                flat_v[a][i, rows, cols] = ratio
            return carry

        lax.fori_loop(0, col_flat // 8, one, 0)
        rows = pl.ds(pl.multiple_of(mine * col_flat, 8), col_flat)
        slot = pl.ds(pl.multiple_of(my_slot * col_flat, 8), col_flat)
        for shard_to in range(shard_count):
            piece = flat_v[a].at[i, :, pl.ds(shard_to * row_block, row_block)]

            def direct():
                send_or_keep(
                    jnp.logical_and(s == shard_to, home == t),
                    piece,
                    back_v[a].at[i, rows, :],
                    back_send.at[position],
                    back_recv.at[position],
                    (shard_to, home),
                )

            def by_stop():
                stop = lax.rem(home + half, tensor_count)
                send_or_keep(
                    jnp.logical_and(s == shard_to, stop == t),
                    piece,
                    back_stop[a].at[i, slot, :],
                    back_send.at[position],
                    bstop_recv.at[position],
                    (shard_to, stop),
                )

            if RELAY_BACK:
                pl.when(same_side)(direct)
                pl.when(jnp.logical_not(same_side))(by_stop)
            else:
                direct()
        pltpu.make_async_copy(first_v[a].at[i], firsts_new[a].at[i], save_m.at[position]).start()
        pltpu.make_async_copy(second_v[a].at[i], seconds_new[a].at[i], save_v.at[position]).start()

    def forward_back(position):
        if not RELAY_BACK:
            return
        a, i = ORDER[position]
        row_block, col_block, col_flat = sizes(a)
        wait_bytes(back_stop[a].at[i], bstop_recv.at[position])
        for y in range(groups):
            rows = pl.ds(
                pl.multiple_of((y * tensor_count + side * half) * col_flat, 8), half * col_flat
            )
            remote(
                back_stop[a].at[i, pl.ds(y * half * col_flat, half * col_flat), :],
                back_v[a].at[i, rows, :],
                bstop_send.at[position],
                back_recv.at[position],
                (s, mate),
            ).start()

    def renew(position):
        a, i = ORDER[position]
        row_block, col_block, col_flat = sizes(a)
        wait_bytes(back_v[a].at[i], back_recv.at[position])
        wait_bytes(weight_v[a].at[i], load_w.at[position])

        def fold(block):
            return jnp.sum((block * block).reshape(row_block // 8, 8, 128), axis=0)

        def one(j, carry):
            span = pl.ds(pl.multiple_of(j * 128, 128), 128)
            weight = weight_v[a][i, :, span]
            update = back_v[a][i, span, :].T + decay_rate * weight
            grad_v[a][i, :, span] = update
            return carry[0] + fold(weight), carry[1] + fold(update)

        zero = jnp.zeros((8, 128), jnp.float32)
        weight_sq, update_sq = lax.fori_loop(0, col_block // 128, one, (zero, zero))
        row = row_of(a, i)
        partial[me, row : row + 1, :] = jnp.sum(weight_sq, axis=0, keepdims=True)
        partial[me, row + 8 : row + 9, :] = jnp.sum(update_sq, axis=0, keepdims=True)
        pltpu.make_async_copy(grad_v[a].at[i], updates[a].at[i], save_u.at[position]).start()

    count = len(ORDER)
    partial[me, :, :] = jnp.zeros((16, 128), jnp.float32)
    turn(0)
    pl.semaphore_wait(barrier, devices - 1)
    send_out(0)
    for position in range(1, count):
        turn(position)
        send_out(position)
    forward_out(0)
    for position in range(count):
        if position + 1 < count:
            forward_out(position + 1)
        moments(position)
    forward_back(0)
    for position in range(count):
        if position + 1 < count:
            forward_back(position + 1)
        renew(position)

    def tell(step, carry):
        other = lax.rem(me + step, devices)
        remote(
            partial.at[me],
            partial.at[me],
            total_sem.at[0],
            total_sem.at[1],
            (other // tensor_count, lax.rem(other, tensor_count)),
        ).start()
        return carry

    lax.fori_loop(1, devices, tell, 0)
    wait_bytes(partial.at[pl.ds(0, devices - 1)], total_sem.at[1])
    total = lax.fori_loop(
        0, devices, lambda d, sofar: sofar + partial[d], jnp.zeros((16, 128), jnp.float32)
    )
    sums_v[...] = total
    pltpu.make_async_copy(sums_v, sums_out, total_sem.at[2]).start()
    wait_bytes(partial.at[pl.ds(0, devices - 1)], total_sem.at[0])

    out_self = home == t if RELAY_OUT else home == t
    stop_self = home == mate
    back_self = home == t
    if RELAY_BACK:
        back_self = jnp.logical_or(home == t, lax.rem(home + half, tensor_count) == t)

    def wait_less(is_less, ref, i, total_rows, piece_rows, sem):
        @pl.when(is_less)
        def _():
            wait_bytes(ref.at[i, pl.ds(0, total_rows - piece_rows), :], sem)

        @pl.when(jnp.logical_not(is_less))
        def _():
            wait_bytes(ref.at[i], sem)

    for position, (a, i) in enumerate(ORDER):
        row_block, col_block, col_flat = sizes(a)
        wait_less(out_self, turned_v[a], i, col_block, col_flat, out_send.at[position])
        wait_less(back_self, turned_v[a], i, col_block, col_flat, back_send.at[position])
        if RELAY_OUT:
            wait_less(stop_self, out_stop[a], i, col_block // 2, col_flat, stop_send.at[position])
        if RELAY_BACK:
            wait_bytes(back_stop[a].at[i], bstop_send.at[position])
        wait_bytes(grad_v[a].at[i], save_u.at[position])
        wait_bytes(first_v[a].at[i], save_m.at[position])
        wait_bytes(second_v[a].at[i], save_v.at[position])
    wait_bytes(sums_v, total_sem.at[2])


def exchange(weights, grads, firsts, seconds, shard_count, tensor_count):
    f32 = jnp.float32
    blocks = [matrix.shape for matrix in weights]
    flats = [matrix.shape for matrix in firsts]
    turned = [(n, c, r) for n, r, c in blocks]
    halves = [(n, c // 2, r) for n, r, c in blocks]
    devices = shard_count * tensor_count
    shapes = blocks + flats + flats + [(16, 128)]
    scratch = []
    for group in (blocks, turned, flats, turned, flats, flats, blocks, halves, halves):
        scratch += [pltpu.VMEM(shape, f32) for shape in group]
    scratch += [pltpu.VMEM((devices, 16, 128), f32), pltpu.VMEM((16, 128), f32)]
    scratch += [pltpu.SemaphoreType.DMA((len(ORDER),))] * 15 + [pltpu.SemaphoreType.DMA((3,))]
    anywhere = pl.BlockSpec(memory_space=pl.ANY)
    return pl.pallas_call(
        functools.partial(exchange_kernel, shard_count, tensor_count),
        out_shape=[jax.ShapeDtypeStruct(shape, f32) for shape in shapes],
        in_specs=[anywhere] * 12,
        out_specs=[anywhere] * 10,
        scratch_shapes=scratch,
        compiler_params=pltpu.CompilerParams(
            collective_id=0, has_side_effects=True, vmem_limit_bytes=56 * 1024 * 1024
        ),
        name="exchange",
    )(*weights, *grads, *firsts, *seconds)


def fits(weights, firsts, shard_count, tensor_count):
    if shard_count % tensor_count or tensor_count % 2:
        return False
    return all(
        matrix.shape[1] % 128 == 0
        and matrix.shape[2] % 128 == 0
        and matrix.shape[2] % (8 * shard_count) == 0
        for matrix in weights
    )


def shards(*arrays):
    shard_count = lax.axis_size("shard")
    tensor_count = lax.axis_size("tensor")
    weights, grads, firsts, seconds = arrays[0:3], arrays[3:6], arrays[6:9], arrays[9:12]
    if not fits(weights, firsts, shard_count, tensor_count):
        return plain(weights, grads, firsts, seconds, shard_count, tensor_count)
    out = exchange(weights, grads, firsts, seconds, shard_count, tensor_count)
    updates, firsts_new, seconds_new, sums = out[0:3], out[3:6], out[6:9], out[9]
    totals = jnp.sum(sums, axis=1)
    trust_ratio = jnp.sqrt(totals[0:7]) / (jnp.sqrt(totals[8:15]) + epsilon)
    return finish(weights, updates, firsts_new, seconds_new, trust_ratio)


def finish(weights, updates, firsts_new, seconds_new, trust_ratio):
    scales = (trust_ratio[0:4], trust_ratio[4:6], trust_ratio[6:7])
    new_weights = [
        weights[position] - learn_rate * scales[position][:, None, None] * updates[position]
        for position in range(3)
    ]
    return (*new_weights, *firsts_new, *seconds_new, trust_ratio)


def plain(weights, grads, firsts, seconds, shard_count, tensor_count):
    row_blocks = [matrix.shape[1] for matrix in weights]
    results = []
    updates = []
    for position in range(3):
        piece = lax.all_to_all(
            lax.all_to_all(
                outbound(grads[position], shard_count, tensor_count),
                "tensor", split_axis=2, concat_axis=1, tiled=True,
            ),
            "shard", split_axis=1, concat_axis=1, tiled=True,
        )
        flat = arrived_flat(piece, row_blocks[position])
        results.append(moment_step(flat, firsts[position], seconds[position]))
        restored = lax.all_to_all(
            lax.all_to_all(
                homebound(results[position][2], row_blocks[position]),
                "shard", split_axis=1, concat_axis=1, tiled=True,
            ),
            "tensor", split_axis=1, concat_axis=2, tiled=True,
        )
        ratio = arrived_block(restored, row_blocks[position])
        updates.append(ratio + decay_rate * weights[position])
    weight_sq = jnp.concatenate([jnp.sum(member * member, axis=(1, 2)) for member in weights])
    update_sq = jnp.concatenate([jnp.sum(member * member, axis=(1, 2)) for member in updates])
    weight_total, update_total = lax.psum((weight_sq, update_sq), ("shard", "tensor"))
    trust_ratio = jnp.sqrt(weight_total) / (jnp.sqrt(update_total) + epsilon)
    return finish(
        weights, updates, [r[0] for r in results], [r[1] for r in results], trust_ratio
    )


def solution(mesh):
    in_specs = (
        P(None, "shard", "tensor"),
        P(None, "shard", "tensor"),
        P(None, "shard", "tensor"),
        P(None, "shard", "tensor"),
        P(None, "shard", "tensor"),
        P(None, "shard", "tensor"),
        P(None, ("shard", "tensor"), None),
        P(None, ("shard", "tensor"), None),
        P(None, ("shard", "tensor"), None),
        P(None, ("shard", "tensor"), None),
        P(None, ("shard", "tensor"), None),
        P(None, ("shard", "tensor"), None),
    )
    out_specs = (
        P(None, "shard", "tensor"),
        P(None, "shard", "tensor"),
        P(None, "shard", "tensor"),
        P(None, ("shard", "tensor"), None),
        P(None, ("shard", "tensor"), None),
        P(None, ("shard", "tensor"), None),
        P(None, ("shard", "tensor"), None),
        P(None, ("shard", "tensor"), None),
        P(None, ("shard", "tensor"), None),
        P(),
    )
    return jax.shard_map(shards, mesh=mesh, in_specs=in_specs, out_specs=out_specs, check_vma=False)
```

```python
import functools

import jax
import jax.numpy as jnp
from jax import lax
from jax.experimental import pallas as pl
from jax.experimental.pallas import tpu as pltpu
from jax.sharding import PartitionSpec as P

MESH = pl.DeviceIdType.MESH
RELAY_OUT = True
RELAY_BACK = False

beta_one = 0.9
beta_two = 0.999
step_number = 10.0
correct_one = 1.0 - beta_one**step_number
correct_two = 1.0 - beta_two**step_number
learn_rate = 0.02
decay_rate = 0.1
epsilon = 1e-06


def moment_step(gradient_t, first_moment, second):
    first_new = beta_one * first_moment + (1.0 - beta_one) * gradient_t
    second_new = beta_two * second + (1.0 - beta_two) * gradient_t * gradient_t
    ratio_value = first_new / correct_one / (jnp.sqrt(second_new / correct_two) + epsilon)
    return (first_new, second_new, ratio_value)


def outbound(block, shard_count, tensor_count):
    stacks, row_block, col_block = block.shape
    groups = shard_count // tensor_count
    col_flat = col_block // shard_count
    turned = jnp.swapaxes(block, 1, 2)
    return turned.reshape(stacks, groups, tensor_count, col_flat * row_block)


def arrived_flat(piece, row_block):
    stacks, shard_count, single, length = piece.shape
    col_flat = length // row_block
    spread = piece.reshape(stacks, shard_count, col_flat, row_block)
    return jnp.transpose(spread, (0, 2, 1, 3)).reshape(stacks, col_flat, shard_count * row_block)


def homebound(flat, row_block):
    stacks, col_flat, rows_all = flat.shape
    shard_count = rows_all // row_block
    spread = flat.reshape(stacks, col_flat, shard_count, row_block)
    return jnp.transpose(spread, (0, 2, 1, 3)).reshape(stacks, shard_count, 1, col_flat * row_block)


def arrived_block(piece, row_block):
    stacks, groups, tensor_count, length = piece.shape
    col_flat = length // row_block
    spread = piece.reshape(stacks, groups * tensor_count * col_flat, row_block)
    return jnp.swapaxes(spread, 1, 2)


ORDER = ((1, 0), (1, 1), (2, 0), (0, 0), (0, 1), (0, 2), (0, 3))


def row_of(array, index):
    return (0, 4, 6)[array] + index


def exchange_kernel(shard_count, tensor_count, *refs):
    weights, grads, firsts, seconds = refs[0:3], refs[3:6], refs[6:9], refs[9:12]
    updates, firsts_new, seconds_new, sums_out = refs[12:15], refs[15:18], refs[18:21], refs[21]
    grad_v, turned_v, flat_v, back_v = refs[22:25], refs[25:28], refs[28:31], refs[31:34]
    first_v, second_v, weight_v = refs[34:37], refs[37:40], refs[40:43]
    out_stop, back_stop = refs[43:46], refs[46:49]
    partial, sums_v = refs[49], refs[50]
    (
        load_g, load_m, load_v, load_w, out_send, out_recv, stop_recv, stop_send,
        back_send, back_recv, bstop_recv, bstop_send, save_u, save_m, save_v, total_sem,
    ) = refs[51:67]

    groups = shard_count // tensor_count
    half = tensor_count // 2
    devices = shard_count * tensor_count
    s, t = lax.axis_index("shard"), lax.axis_index("tensor")
    me = s * tensor_count + t
    mate = lax.rem(t + half, tensor_count)
    side = t // half
    home = s // groups
    mine = lax.rem(s, groups) * tensor_count + t
    my_slot = lax.rem(s, groups) * half + lax.rem(t, half)
    same_side = home // half == side

    for position, (a, i) in enumerate(ORDER):
        pltpu.make_async_copy(grads[a].at[i], grad_v[a].at[i], load_g.at[position]).start()
    for position, (a, i) in enumerate(ORDER):
        pltpu.make_async_copy(firsts[a].at[i], first_v[a].at[i], load_m.at[position]).start()
        pltpu.make_async_copy(seconds[a].at[i], second_v[a].at[i], load_v.at[position]).start()
        pltpu.make_async_copy(weights[a].at[i], weight_v[a].at[i], load_w.at[position]).start()

    barrier = pltpu.get_barrier_semaphore()

    def greet(step, carry):
        other = lax.rem(me + step, devices)
        pl.semaphore_signal(
            barrier,
            inc=1,
            device_id=(other // tensor_count, lax.rem(other, tensor_count)),
            device_id_type=MESH,
        )
        return carry

    lax.fori_loop(1, devices, greet, 0)

    def sizes(a):
        row_block, col_block = weights[a].shape[1:]
        return row_block, col_block, col_block // shard_count

    def remote(src, dst, send, recv, device):
        return pltpu.make_async_remote_copy(
            src_ref=src, dst_ref=dst, send_sem=send, recv_sem=recv,
            device_id=device, device_id_type=MESH,
        )

    def send_or_keep(is_me, src, dst, send, recv, device):
        @pl.when(is_me)
        def _():
            pltpu.make_async_copy(src, dst, recv).start()

        @pl.when(jnp.logical_not(is_me))
        def _():
            remote(src, dst, send, recv, device).start()

    def wait_bytes(ref, sem):
        pltpu.make_async_copy(ref, ref, sem).wait()

    def turn(position):
        a, i = ORDER[position]
        row_block, col_block, col_flat = sizes(a)
        wait_bytes(grad_v[a].at[i], load_g.at[position])

        def one(j, carry):
            span = pl.ds(pl.multiple_of(j * 128, 128), 128)
            turned_v[a][i, span, :] = grad_v[a][i, :, span].T
            return carry

        lax.fori_loop(0, col_block // 128, one, 0)

    def send_out(position):
        a, i = ORDER[position]
        row_block, col_block, col_flat = sizes(a)
        land = pl.ds(pl.multiple_of(s * row_block, 128), row_block)
        send, recv = out_send.at[position], out_recv.at[position]
        if RELAY_OUT:
            other_side = mate // half
            for y in range(groups):
                rows = pl.ds(
                    pl.multiple_of((y * tensor_count + other_side * half) * col_flat, 8),
                    half * col_flat,
                )
                remote(
                    turned_v[a].at[i, rows, :],
                    out_stop[a].at[i, pl.ds(y * half * col_flat, half * col_flat), :],
                    send,
                    stop_recv.at[position],
                    (s, mate),
                ).start()
            for y in range(groups):
                for core in range(half):
                    target = side * half + core
                    k = y * tensor_count + target
                    rows = pl.ds(pl.multiple_of(k * col_flat, 8), col_flat)
                    shard_to = groups * t + y
                    send_or_keep(
                        jnp.logical_and(shard_to == s, target == t),
                        turned_v[a].at[i, rows, :],
                        flat_v[a].at[i, :, land],
                        send,
                        recv,
                        (shard_to, target),
                    )
        else:
            for k in range(shard_count):
                shard_to, target = groups * t + k // tensor_count, k % tensor_count
                send_or_keep(
                    jnp.logical_and(shard_to == s, target == t),
                    turned_v[a].at[i, pl.ds(k * col_flat, col_flat), :],
                    flat_v[a].at[i, :, land],
                    send,
                    recv,
                    (shard_to, target),
                )

    def forward_out(position):
        if not RELAY_OUT:
            return
        a, i = ORDER[position]
        row_block, col_block, col_flat = sizes(a)
        wait_bytes(out_stop[a].at[i], stop_recv.at[position])
        land = pl.ds(pl.multiple_of(s * row_block, 128), row_block)
        for y in range(groups):
            for core in range(half):
                target = side * half + core
                shard_to = groups * mate + y
                send_or_keep(
                    jnp.logical_and(shard_to == s, target == t),
                    out_stop[a].at[i, pl.ds((y * half + core) * col_flat, col_flat), :],
                    flat_v[a].at[i, :, land],
                    stop_send.at[position],
                    out_recv.at[position],
                    (shard_to, target),
                )

    def moments(position):
        a, i = ORDER[position]
        row_block, col_block, col_flat = sizes(a)
        wait_bytes(flat_v[a].at[i], out_recv.at[position])
        wait_bytes(first_v[a].at[i], load_m.at[position])
        wait_bytes(second_v[a].at[i], load_v.at[position])
        length = shard_count * row_block
        width = 1024 if length % 1024 == 0 else row_block

        def one(j, carry):
            rows = pl.ds(pl.multiple_of(j * 8, 8), 8)
            for at in range(0, length, width):
                cols = pl.ds(at, width)
                first_new, second_new, ratio = moment_step(
                    flat_v[a][i, rows, cols], first_v[a][i, rows, cols], second_v[a][i, rows, cols]
                )
                first_v[a][i, rows, cols] = first_new
                second_v[a][i, rows, cols] = second_new
                flat_v[a][i, rows, cols] = ratio
            return carry

        lax.fori_loop(0, col_flat // 8, one, 0)
        rows = pl.ds(pl.multiple_of(mine * col_flat, 8), col_flat)
        slot = pl.ds(pl.multiple_of(my_slot * col_flat, 8), col_flat)
        for shard_to in range(shard_count):
            piece = flat_v[a].at[i, :, pl.ds(shard_to * row_block, row_block)]

            def direct():
                send_or_keep(
                    jnp.logical_and(s == shard_to, home == t),
                    piece,
                    back_v[a].at[i, rows, :],
                    back_send.at[position],
                    back_recv.at[position],
                    (shard_to, home),
                )

            def by_stop():
                stop = lax.rem(home + half, tensor_count)
                send_or_keep(
                    jnp.logical_and(s == shard_to, stop == t),
                    piece,
                    back_stop[a].at[i, slot, :],
                    back_send.at[position],
                    bstop_recv.at[position],
                    (shard_to, stop),
                )

            if RELAY_BACK:
                pl.when(same_side)(direct)
                pl.when(jnp.logical_not(same_side))(by_stop)
            else:
                direct()
        pltpu.make_async_copy(first_v[a].at[i], firsts_new[a].at[i], save_m.at[position]).start()
        pltpu.make_async_copy(second_v[a].at[i], seconds_new[a].at[i], save_v.at[position]).start()

    def forward_back(position):
        if not RELAY_BACK:
            return
        a, i = ORDER[position]
        row_block, col_block, col_flat = sizes(a)
        wait_bytes(back_stop[a].at[i], bstop_recv.at[position])
        for y in range(groups):
            rows = pl.ds(
                pl.multiple_of((y * tensor_count + side * half) * col_flat, 8), half * col_flat
            )
            remote(
                back_stop[a].at[i, pl.ds(y * half * col_flat, half * col_flat), :],
                back_v[a].at[i, rows, :],
                bstop_send.at[position],
                back_recv.at[position],
                (s, mate),
            ).start()

    def renew(position):
        a, i = ORDER[position]
        row_block, col_block, col_flat = sizes(a)
        wait_bytes(back_v[a].at[i], back_recv.at[position])
        wait_bytes(weight_v[a].at[i], load_w.at[position])

        def fold(block):
            return jnp.sum((block * block).reshape(row_block // 8, 8, 128), axis=0)

        def one(j, carry):
            span = pl.ds(pl.multiple_of(j * 128, 128), 128)
            weight = weight_v[a][i, :, span]
            update = back_v[a][i, span, :].T + decay_rate * weight
            grad_v[a][i, :, span] = update
            return carry[0] + fold(weight), carry[1] + fold(update)

        zero = jnp.zeros((8, 128), jnp.float32)
        weight_sq, update_sq = lax.fori_loop(0, col_block // 128, one, (zero, zero))
        row = row_of(a, i)
        partial[me, row : row + 1, :] = jnp.sum(weight_sq, axis=0, keepdims=True)
        partial[me, row + 8 : row + 9, :] = jnp.sum(update_sq, axis=0, keepdims=True)
        pltpu.make_async_copy(grad_v[a].at[i], updates[a].at[i], save_u.at[position]).start()

    count = len(ORDER)
    partial[me, :, :] = jnp.zeros((16, 128), jnp.float32)
    turn(0)
    pl.semaphore_wait(barrier, devices - 1)
    send_out(0)
    for position in range(1, count):
        turn(position)
        send_out(position)
    forward_out(0)
    for position in range(count):
        if position + 1 < count:
            forward_out(position + 1)
        moments(position)
    forward_back(0)
    for position in range(count):
        if position + 1 < count:
            forward_back(position + 1)
        renew(position)

    def tell(step, carry):
        other = lax.rem(me + step, devices)
        remote(
            partial.at[me],
            partial.at[me],
            total_sem.at[0],
            total_sem.at[1],
            (other // tensor_count, lax.rem(other, tensor_count)),
        ).start()
        return carry

    lax.fori_loop(1, devices, tell, 0)
    wait_bytes(partial.at[pl.ds(0, devices - 1)], total_sem.at[1])
    total = lax.fori_loop(
        0, devices, lambda d, sofar: sofar + partial[d], jnp.zeros((16, 128), jnp.float32)
    )
    sums_v[...] = total
    pltpu.make_async_copy(sums_v, sums_out, total_sem.at[2]).start()
    wait_bytes(partial.at[pl.ds(0, devices - 1)], total_sem.at[0])

    out_self = home == t if RELAY_OUT else home == t
    stop_self = home == mate
    back_self = home == t
    if RELAY_BACK:
        back_self = jnp.logical_or(home == t, lax.rem(home + half, tensor_count) == t)

    def wait_less(is_less, ref, i, total_rows, piece_rows, sem):
        @pl.when(is_less)
        def _():
            wait_bytes(ref.at[i, pl.ds(0, total_rows - piece_rows), :], sem)

        @pl.when(jnp.logical_not(is_less))
        def _():
            wait_bytes(ref.at[i], sem)

    for position, (a, i) in enumerate(ORDER):
        row_block, col_block, col_flat = sizes(a)
        wait_less(out_self, turned_v[a], i, col_block, col_flat, out_send.at[position])
        wait_less(back_self, turned_v[a], i, col_block, col_flat, back_send.at[position])
        if RELAY_OUT:
            wait_less(stop_self, out_stop[a], i, col_block // 2, col_flat, stop_send.at[position])
        if RELAY_BACK:
            wait_bytes(back_stop[a].at[i], bstop_send.at[position])
        wait_bytes(grad_v[a].at[i], save_u.at[position])
        wait_bytes(first_v[a].at[i], save_m.at[position])
        wait_bytes(second_v[a].at[i], save_v.at[position])
    wait_bytes(sums_v, total_sem.at[2])


def exchange(weights, grads, firsts, seconds, shard_count, tensor_count):
    f32 = jnp.float32
    blocks = [matrix.shape for matrix in weights]
    flats = [matrix.shape for matrix in firsts]
    turned = [(n, c, r) for n, r, c in blocks]
    halves = [(n, c // 2, r) for n, r, c in blocks]
    devices = shard_count * tensor_count
    shapes = blocks + flats + flats + [(16, 128)]
    scratch = []
    for group in (blocks, turned, flats, turned, flats, flats, blocks, halves, halves):
        scratch += [pltpu.VMEM(shape, f32) for shape in group]
    scratch += [pltpu.VMEM((devices, 16, 128), f32), pltpu.VMEM((16, 128), f32)]
    scratch += [pltpu.SemaphoreType.DMA((len(ORDER),))] * 15 + [pltpu.SemaphoreType.DMA((3,))]
    anywhere = pl.BlockSpec(memory_space=pl.ANY)
    return pl.pallas_call(
        functools.partial(exchange_kernel, shard_count, tensor_count),
        out_shape=[jax.ShapeDtypeStruct(shape, f32) for shape in shapes],
        in_specs=[anywhere] * 12,
        out_specs=[anywhere] * 10,
        scratch_shapes=scratch,
        compiler_params=pltpu.CompilerParams(
            collective_id=0, has_side_effects=True, vmem_limit_bytes=56 * 1024 * 1024
        ),
        name="exchange",
    )(*weights, *grads, *firsts, *seconds)


def fits(weights, firsts, shard_count, tensor_count):
    if shard_count % tensor_count or tensor_count % 2:
        return False
    return all(
        matrix.shape[1] % 128 == 0
        and matrix.shape[2] % 128 == 0
        and matrix.shape[2] % (8 * shard_count) == 0
        for matrix in weights
    )


def shards(*arrays):
    shard_count = lax.axis_size("shard")
    tensor_count = lax.axis_size("tensor")
    weights, grads, firsts, seconds = arrays[0:3], arrays[3:6], arrays[6:9], arrays[9:12]
    if not fits(weights, firsts, shard_count, tensor_count):
        return plain(weights, grads, firsts, seconds, shard_count, tensor_count)
    out = exchange(weights, grads, firsts, seconds, shard_count, tensor_count)
    updates, firsts_new, seconds_new, sums = out[0:3], out[3:6], out[6:9], out[9]
    totals = jnp.sum(sums, axis=1)
    trust_ratio = jnp.sqrt(totals[0:7]) / (jnp.sqrt(totals[8:15]) + epsilon)
    return finish(weights, updates, firsts_new, seconds_new, trust_ratio)


def finish(weights, updates, firsts_new, seconds_new, trust_ratio):
    scales = (trust_ratio[0:4], trust_ratio[4:6], trust_ratio[6:7])
    new_weights = [
        weights[position] - learn_rate * scales[position][:, None, None] * updates[position]
        for position in range(3)
    ]
    return (*new_weights, *firsts_new, *seconds_new, trust_ratio)


def plain(weights, grads, firsts, seconds, shard_count, tensor_count):
    row_blocks = [matrix.shape[1] for matrix in weights]
    results = []
    updates = []
    for position in range(3):
        piece = lax.all_to_all(
            lax.all_to_all(
                outbound(grads[position], shard_count, tensor_count),
                "tensor", split_axis=2, concat_axis=1, tiled=True,
            ),
            "shard", split_axis=1, concat_axis=1, tiled=True,
        )
        flat = arrived_flat(piece, row_blocks[position])
        results.append(moment_step(flat, firsts[position], seconds[position]))
        restored = lax.all_to_all(
            lax.all_to_all(
                homebound(results[position][2], row_blocks[position]),
                "shard", split_axis=1, concat_axis=1, tiled=True,
            ),
            "tensor", split_axis=1, concat_axis=2, tiled=True,
        )
        ratio = arrived_block(restored, row_blocks[position])
        updates.append(ratio + decay_rate * weights[position])
    weight_sq = jnp.concatenate([jnp.sum(member * member, axis=(1, 2)) for member in weights])
    update_sq = jnp.concatenate([jnp.sum(member * member, axis=(1, 2)) for member in updates])
    weight_total, update_total = lax.psum((weight_sq, update_sq), ("shard", "tensor"))
    trust_ratio = jnp.sqrt(weight_total) / (jnp.sqrt(update_total) + epsilon)
    return finish(
        weights, updates, [r[0] for r in results], [r[1] for r in results], trust_ratio
    )


def solution(mesh):
    in_specs = (
        P(None, "shard", "tensor"),
        P(None, "shard", "tensor"),
        P(None, "shard", "tensor"),
        P(None, "shard", "tensor"),
        P(None, "shard", "tensor"),
        P(None, "shard", "tensor"),
        P(None, ("shard", "tensor"), None),
        P(None, ("shard", "tensor"), None),
        P(None, ("shard", "tensor"), None),
        P(None, ("shard", "tensor"), None),
        P(None, ("shard", "tensor"), None),
        P(None, ("shard", "tensor"), None),
    )
    out_specs = (
        P(None, "shard", "tensor"),
        P(None, "shard", "tensor"),
        P(None, "shard", "tensor"),
        P(None, ("shard", "tensor"), None),
        P(None, ("shard", "tensor"), None),
        P(None, ("shard", "tensor"), None),
        P(None, ("shard", "tensor"), None),
        P(None, ("shard", "tensor"), None),
        P(None, ("shard", "tensor"), None),
        P(),
    )
    return jax.shard_map(shards, mesh=mesh, in_specs=in_specs, out_specs=out_specs, check_vma=False)
```

```python
import functools

import jax
import jax.numpy as jnp
from jax import lax
from jax.experimental import pallas as pl
from jax.experimental.pallas import tpu as pltpu
from jax.sharding import PartitionSpec as P

MESH = pl.DeviceIdType.MESH

beta_one = 0.9
beta_two = 0.999
step_number = 10.0
correct_one = 1.0 - beta_one**step_number
correct_two = 1.0 - beta_two**step_number
learn_rate = 0.02
decay_rate = 0.1
epsilon = 1e-06


def moment_step(gradient_t, first_moment, second):
    first_new = beta_one * first_moment + (1.0 - beta_one) * gradient_t
    second_new = beta_two * second + (1.0 - beta_two) * gradient_t * gradient_t
    ratio_value = first_new / correct_one / (jnp.sqrt(second_new / correct_two) + epsilon)
    return (first_new, second_new, ratio_value)


def outbound(block, shard_count, tensor_count):
    stacks, row_block, col_block = block.shape
    groups = shard_count // tensor_count
    col_flat = col_block // shard_count
    turned = jnp.swapaxes(block, 1, 2)
    return turned.reshape(stacks, groups, tensor_count, col_flat * row_block)


def arrived_flat(piece, row_block):
    stacks, shard_count, single, length = piece.shape
    col_flat = length // row_block
    spread = piece.reshape(stacks, shard_count, col_flat, row_block)
    return jnp.transpose(spread, (0, 2, 1, 3)).reshape(stacks, col_flat, shard_count * row_block)


def homebound(flat, row_block):
    stacks, col_flat, rows_all = flat.shape
    shard_count = rows_all // row_block
    spread = flat.reshape(stacks, col_flat, shard_count, row_block)
    return jnp.transpose(spread, (0, 2, 1, 3)).reshape(stacks, shard_count, 1, col_flat * row_block)


def arrived_block(piece, row_block):
    stacks, groups, tensor_count, length = piece.shape
    col_flat = length // row_block
    spread = piece.reshape(stacks, groups * tensor_count * col_flat, row_block)
    return jnp.swapaxes(spread, 1, 2)


ORDER = ((0, 0), (1, 0), (1, 1), (2, 0), (0, 1), (0, 2), (0, 3))


def row_of(array, index):
    return (0, 4, 6)[array] + index


def exchange_kernel(shard_count, tensor_count, *refs):
    weights, grads, firsts, seconds = refs[0:3], refs[3:6], refs[6:9], refs[9:12]
    updates, firsts_new, seconds_new, sums_out = refs[12:15], refs[15:18], refs[18:21], refs[21]
    grad_v, turned_v, flat_v, back_v = refs[22:25], refs[25:28], refs[28:31], refs[31:34]
    first_v, second_v, weight_v = refs[34:37], refs[37:40], refs[40:43]
    out_stop = refs[43:46]
    partial, sums_v = refs[46], refs[47]
    (
        load_g, load_m, load_v, load_w, out_send, out_recv, stop_recv, stop_send,
        back_send, back_recv, save_u, save_m, save_v, total_sem,
    ) = refs[48:62]

    groups = shard_count // tensor_count
    half = tensor_count // 2
    devices = shard_count * tensor_count
    s, t = lax.axis_index("shard"), lax.axis_index("tensor")
    me = s * tensor_count + t
    mate = lax.rem(t + half, tensor_count)
    side = t // half
    home = s // groups
    mine = lax.rem(s, groups) * tensor_count + t
    turn_from = s + lax.rem(t, half) * (shard_count // half)

    for position, (a, i) in enumerate(ORDER):
        pltpu.make_async_copy(grads[a].at[i], grad_v[a].at[i], load_g.at[position]).start()
    for position, (a, i) in enumerate(ORDER):
        pltpu.make_async_copy(firsts[a].at[i], first_v[a].at[i], load_m.at[position]).start()
        pltpu.make_async_copy(seconds[a].at[i], second_v[a].at[i], load_v.at[position]).start()
        pltpu.make_async_copy(weights[a].at[i], weight_v[a].at[i], load_w.at[position]).start()

    barrier = pltpu.get_barrier_semaphore()

    def greet(step, carry):
        other = lax.rem(me + step, devices)
        pl.semaphore_signal(
            barrier,
            inc=1,
            device_id=(other // tensor_count, lax.rem(other, tensor_count)),
            device_id_type=MESH,
        )
        return carry

    lax.fori_loop(1, devices, greet, 0)

    def sizes(a):
        row_block, col_block = weights[a].shape[1:]
        return row_block, col_block, col_block // shard_count

    def remote(src, dst, send, recv, device):
        return pltpu.make_async_remote_copy(
            src_ref=src, dst_ref=dst, send_sem=send, recv_sem=recv,
            device_id=device, device_id_type=MESH,
        )

    def send_or_keep(is_me, src, dst, send, recv, device):
        @pl.when(is_me)
        def _():
            pltpu.make_async_copy(src, dst, recv).start()

        @pl.when(jnp.logical_not(is_me))
        def _():
            remote(src, dst, send, recv, device).start()

    def wait_bytes(ref, sem):
        pltpu.make_async_copy(ref, ref, sem).wait()

    def turn(position):
        a, i = ORDER[position]
        row_block, col_block, col_flat = sizes(a)
        wait_bytes(grad_v[a].at[i], load_g.at[position])

        def one(j, carry):
            span = pl.ds(pl.multiple_of(j * 128, 128), 128)
            turned_v[a][i, span, :] = grad_v[a][i, :, span].T
            return carry

        lax.fori_loop(0, col_block // 128, one, 0)

    def send_mate(position):
        a, i = ORDER[position]
        row_block, col_block, col_flat = sizes(a)
        other_side = mate // half
        for y in range(groups):
            rows = pl.ds(
                pl.multiple_of((y * tensor_count + other_side * half) * col_flat, 8),
                half * col_flat,
            )
            remote(
                turned_v[a].at[i, rows, :],
                out_stop[a].at[i, pl.ds(y * half * col_flat, half * col_flat), :],
                out_send.at[position],
                stop_recv.at[position],
                (s, mate),
            ).start()

    def send_out(position):
        a, i = ORDER[position]
        row_block, col_block, col_flat = sizes(a)
        land = pl.ds(pl.multiple_of(s * row_block, 128), row_block)
        for y in range(groups):
            for core in range(half):
                target = side * half + core
                k = y * tensor_count + target
                shard_to = groups * t + y
                send_or_keep(
                    jnp.logical_and(shard_to == s, target == t),
                    turned_v[a].at[i, pl.ds(pl.multiple_of(k * col_flat, 8), col_flat), :],
                    flat_v[a].at[i, :, land],
                    out_send.at[position],
                    out_recv.at[position],
                    (shard_to, target),
                )

    def forward_out(position):
        a, i = ORDER[position]
        row_block, col_block, col_flat = sizes(a)
        wait_bytes(out_stop[a].at[i], stop_recv.at[position])
        land = pl.ds(pl.multiple_of(s * row_block, 128), row_block)
        for y in range(groups):
            for core in range(half):
                target = side * half + core
                shard_to = groups * mate + y
                send_or_keep(
                    jnp.logical_and(shard_to == s, target == t),
                    out_stop[a].at[i, pl.ds((y * half + core) * col_flat, col_flat), :],
                    flat_v[a].at[i, :, land],
                    stop_send.at[position],
                    out_recv.at[position],
                    (shard_to, target),
                )

    def moments(position):
        a, i = ORDER[position]
        row_block, col_block, col_flat = sizes(a)
        wait_bytes(flat_v[a].at[i], out_recv.at[position])
        wait_bytes(first_v[a].at[i], load_m.at[position])
        wait_bytes(second_v[a].at[i], load_v.at[position])
        length = shard_count * row_block
        width = 1024 if length % 1024 == 0 else row_block

        def one(j, carry):
            rows = pl.ds(pl.multiple_of(j * 8, 8), 8)
            for at in range(0, length, width):
                cols = pl.ds(at, width)
                first_new, second_new, ratio = moment_step(
                    flat_v[a][i, rows, cols], first_v[a][i, rows, cols], second_v[a][i, rows, cols]
                )
                first_v[a][i, rows, cols] = first_new
                second_v[a][i, rows, cols] = second_new
                flat_v[a][i, rows, cols] = ratio
            return carry

        lax.fori_loop(0, col_flat // 8, one, 0)
        rows = pl.ds(pl.multiple_of(mine * col_flat, 8), col_flat)
        for step in range(shard_count):
            shard_to = lax.rem(turn_from + step, shard_count)
            send_or_keep(
                jnp.logical_and(s == shard_to, home == t),
                flat_v[a].at[i, :, pl.ds(pl.multiple_of(shard_to * row_block, 128), row_block)],
                back_v[a].at[i, rows, :],
                back_send.at[position],
                back_recv.at[position],
                (shard_to, home),
            )
        pltpu.make_async_copy(first_v[a].at[i], firsts_new[a].at[i], save_m.at[position]).start()
        pltpu.make_async_copy(second_v[a].at[i], seconds_new[a].at[i], save_v.at[position]).start()

    def renew(position):
        a, i = ORDER[position]
        row_block, col_block, col_flat = sizes(a)
        wait_bytes(back_v[a].at[i], back_recv.at[position])
        wait_bytes(weight_v[a].at[i], load_w.at[position])

        def fold(block):
            return jnp.sum((block * block).reshape(row_block // 8, 8, 128), axis=0)

        def one(j, carry):
            span = pl.ds(pl.multiple_of(j * 128, 128), 128)
            weight = weight_v[a][i, :, span]
            update = back_v[a][i, span, :].T + decay_rate * weight
            grad_v[a][i, :, span] = update
            return carry[0] + fold(weight), carry[1] + fold(update)

        zero = jnp.zeros((8, 128), jnp.float32)
        weight_sq, update_sq = lax.fori_loop(0, col_block // 128, one, (zero, zero))
        row = row_of(a, i)
        partial[me, row : row + 1, :] = jnp.sum(weight_sq, axis=0, keepdims=True)
        partial[me, row + 8 : row + 9, :] = jnp.sum(update_sq, axis=0, keepdims=True)
        pltpu.make_async_copy(grad_v[a].at[i], updates[a].at[i], save_u.at[position]).start()

    count = len(ORDER)
    partial[me, :, :] = jnp.zeros((16, 128), jnp.float32)
    turn(0)
    pl.semaphore_wait(barrier, devices - 1)
    send_mate(0)
    turn(1)
    send_mate(1)
    send_out(0)
    for position in range(count):
        forward_out(position)
        if position + 2 < count:
            turn(position + 2)
            send_mate(position + 2)
        if position + 1 < count:
            send_out(position + 1)
    for position in range(count):
        moments(position)
    for position in range(count):
        renew(position)

    def tell(step, carry):
        other = lax.rem(me + step, devices)
        remote(
            partial.at[me],
            partial.at[me],
            total_sem.at[0],
            total_sem.at[1],
            (other // tensor_count, lax.rem(other, tensor_count)),
        ).start()
        return carry

    lax.fori_loop(1, devices, tell, 0)
    wait_bytes(partial.at[pl.ds(0, devices - 1)], total_sem.at[1])
    total = lax.fori_loop(
        0, devices, lambda d, sofar: sofar + partial[d], jnp.zeros((16, 128), jnp.float32)
    )
    sums_v[...] = total
    pltpu.make_async_copy(sums_v, sums_out, total_sem.at[2]).start()
    wait_bytes(partial.at[pl.ds(0, devices - 1)], total_sem.at[0])

    to_self, stop_self = home == t, home == mate

    def wait_less(is_less, ref, i, total_rows, piece_rows, sem):
        @pl.when(is_less)
        def _():
            wait_bytes(ref.at[i, pl.ds(0, total_rows - piece_rows), :], sem)

        @pl.when(jnp.logical_not(is_less))
        def _():
            wait_bytes(ref.at[i], sem)

    for position, (a, i) in enumerate(ORDER):
        row_block, col_block, col_flat = sizes(a)
        wait_less(to_self, turned_v[a], i, col_block, col_flat, out_send.at[position])
        wait_less(to_self, turned_v[a], i, col_block, col_flat, back_send.at[position])
        wait_less(stop_self, out_stop[a], i, col_block // 2, col_flat, stop_send.at[position])
        wait_bytes(grad_v[a].at[i], save_u.at[position])
        wait_bytes(first_v[a].at[i], save_m.at[position])
        wait_bytes(second_v[a].at[i], save_v.at[position])
    wait_bytes(sums_v, total_sem.at[2])


def exchange(weights, grads, firsts, seconds, shard_count, tensor_count):
    f32 = jnp.float32
    blocks = [matrix.shape for matrix in weights]
    flats = [matrix.shape for matrix in firsts]
    turned = [(n, c, r) for n, r, c in blocks]
    halves = [(n, c // 2, r) for n, r, c in blocks]
    devices = shard_count * tensor_count
    shapes = blocks + flats + flats + [(16, 128)]
    scratch = []
    for group in (blocks, turned, flats, turned, flats, flats, blocks, halves):
        scratch += [pltpu.VMEM(shape, f32) for shape in group]
    scratch += [pltpu.VMEM((devices, 16, 128), f32), pltpu.VMEM((16, 128), f32)]
    scratch += [pltpu.SemaphoreType.DMA((len(ORDER),))] * 13 + [pltpu.SemaphoreType.DMA((3,))]
    anywhere = pl.BlockSpec(memory_space=pl.ANY)
    return pl.pallas_call(
        functools.partial(exchange_kernel, shard_count, tensor_count),
        out_shape=[jax.ShapeDtypeStruct(shape, f32) for shape in shapes],
        in_specs=[anywhere] * 12,
        out_specs=[anywhere] * 10,
        scratch_shapes=scratch,
        compiler_params=pltpu.CompilerParams(
            collective_id=0, has_side_effects=True, vmem_limit_bytes=56 * 1024 * 1024
        ),
        name="exchange",
    )(*weights, *grads, *firsts, *seconds)


def step_kernel(*refs):
    weights, updates, firsts, seconds, sums = refs[0:3], refs[3:6], refs[6:9], refs[9:12], refs[12]
    weights_new, firsts_new, seconds_new, trust = refs[13:16], refs[16:19], refs[19:22], refs[22]
    weight_v, update_v, first_v, second_v = refs[23:26], refs[26:29], refs[29:32], refs[32:35]
    load_w, load_u, load_m, load_v, save_w, save_m, save_v = refs[35:42]
    for position, (a, i) in enumerate(ORDER):
        pltpu.make_async_copy(updates[a].at[i], update_v[a].at[i], load_u.at[position]).start()
        pltpu.make_async_copy(weights[a].at[i], weight_v[a].at[i], load_w.at[position]).start()
        pltpu.make_async_copy(firsts[a].at[i], first_v[a].at[i], load_m.at[position]).start()
        pltpu.make_async_copy(seconds[a].at[i], second_v[a].at[i], load_v.at[position]).start()
    totals = jnp.sum(sums[...], axis=1, keepdims=True)
    ratio = jnp.sqrt(totals[0:8]) / (jnp.sqrt(totals[8:16]) + epsilon)
    trust[...] = jnp.broadcast_to(ratio, (8, 128))

    def wait_bytes(ref, sem):
        pltpu.make_async_copy(ref, ref, sem).wait()

    for position, (a, i) in enumerate(ORDER):
        row = row_of(a, i)
        scale = learn_rate * trust[row : row + 1, 0:1]
        wait_bytes(update_v[a].at[i], load_u.at[position])
        wait_bytes(weight_v[a].at[i], load_w.at[position])

        def one(j, carry):
            rows = pl.ds(pl.multiple_of(j * 8, 8), 8)
            weight_v[a][i, rows, :] = weight_v[a][i, rows, :] - scale * update_v[a][i, rows, :]
            return carry

        lax.fori_loop(0, weights[a].shape[1] // 8, one, 0)
        pltpu.make_async_copy(weight_v[a].at[i], weights_new[a].at[i], save_w.at[position]).start()
        wait_bytes(first_v[a].at[i], load_m.at[position])
        pltpu.make_async_copy(first_v[a].at[i], firsts_new[a].at[i], save_m.at[position]).start()
        wait_bytes(second_v[a].at[i], load_v.at[position])
        pltpu.make_async_copy(second_v[a].at[i], seconds_new[a].at[i], save_v.at[position]).start()
    for position, (a, i) in enumerate(ORDER):
        wait_bytes(weight_v[a].at[i], save_w.at[position])
        wait_bytes(first_v[a].at[i], save_m.at[position])
        wait_bytes(second_v[a].at[i], save_v.at[position])


def apply_step(weights, updates, firsts, seconds, sums):
    f32 = jnp.float32
    blocks = [matrix.shape for matrix in weights]
    flats = [matrix.shape for matrix in firsts]
    anywhere = pl.BlockSpec(memory_space=pl.ANY)
    whole = pl.BlockSpec(memory_space=pltpu.VMEM)
    scratch = [pltpu.VMEM(shape, f32) for shape in blocks + blocks + flats + flats]
    scratch += [pltpu.SemaphoreType.DMA((len(ORDER),))] * 7
    return pl.pallas_call(
        step_kernel,
        out_shape=[
            jax.ShapeDtypeStruct(shape, f32) for shape in blocks + flats + flats + [(8, 128)]
        ],
        in_specs=[anywhere] * 12 + [whole],
        out_specs=[anywhere] * 9 + [whole],
        scratch_shapes=scratch,
        compiler_params=pltpu.CompilerParams(vmem_limit_bytes=48 * 1024 * 1024),
        name="apply_step",
    )(*weights, *updates, *firsts, *seconds, sums)


def fits(weights, firsts, shard_count, tensor_count):
    if shard_count % tensor_count or tensor_count % 2:
        return False
    return all(
        matrix.shape[1] % 128 == 0
        and matrix.shape[2] % 128 == 0
        and matrix.shape[2] % (8 * shard_count) == 0
        for matrix in weights
    )


def shards(*arrays):
    shard_count = lax.axis_size("shard")
    tensor_count = lax.axis_size("tensor")
    weights, grads, firsts, seconds = arrays[0:3], arrays[3:6], arrays[6:9], arrays[9:12]
    if not fits(weights, firsts, shard_count, tensor_count):
        return plain(weights, grads, firsts, seconds, shard_count, tensor_count)
    out = exchange(weights, grads, firsts, seconds, shard_count, tensor_count)
    updates, firsts_new, seconds_new, sums = out[0:3], out[3:6], out[6:9], out[9]
    done = apply_step(weights, updates, firsts_new, seconds_new, sums)
    return (*done[0:9], done[9][0:7, 0])


def finish(weights, updates, firsts_new, seconds_new, trust_ratio):
    scales = (trust_ratio[0:4], trust_ratio[4:6], trust_ratio[6:7])
    new_weights = [
        weights[position] - learn_rate * scales[position][:, None, None] * updates[position]
        for position in range(3)
    ]
    return (*new_weights, *firsts_new, *seconds_new, trust_ratio)


def plain(weights, grads, firsts, seconds, shard_count, tensor_count):
    row_blocks = [matrix.shape[1] for matrix in weights]
    results = []
    updates = []
    for position in range(3):
        piece = lax.all_to_all(
            lax.all_to_all(
                outbound(grads[position], shard_count, tensor_count),
                "tensor", split_axis=2, concat_axis=1, tiled=True,
            ),
            "shard", split_axis=1, concat_axis=1, tiled=True,
        )
        flat = arrived_flat(piece, row_blocks[position])
        results.append(moment_step(flat, firsts[position], seconds[position]))
        restored = lax.all_to_all(
            lax.all_to_all(
                homebound(results[position][2], row_blocks[position]),
                "shard", split_axis=1, concat_axis=1, tiled=True,
            ),
            "tensor", split_axis=1, concat_axis=2, tiled=True,
        )
        ratio = arrived_block(restored, row_blocks[position])
        updates.append(ratio + decay_rate * weights[position])
    weight_sq = jnp.concatenate([jnp.sum(member * member, axis=(1, 2)) for member in weights])
    update_sq = jnp.concatenate([jnp.sum(member * member, axis=(1, 2)) for member in updates])
    weight_total, update_total = lax.psum((weight_sq, update_sq), ("shard", "tensor"))
    trust_ratio = jnp.sqrt(weight_total) / (jnp.sqrt(update_total) + epsilon)
    return finish(
        weights, updates, [r[0] for r in results], [r[1] for r in results], trust_ratio
    )


def solution(mesh):
    in_specs = (
        P(None, "shard", "tensor"),
        P(None, "shard", "tensor"),
        P(None, "shard", "tensor"),
        P(None, "shard", "tensor"),
        P(None, "shard", "tensor"),
        P(None, "shard", "tensor"),
        P(None, ("shard", "tensor"), None),
        P(None, ("shard", "tensor"), None),
        P(None, ("shard", "tensor"), None),
        P(None, ("shard", "tensor"), None),
        P(None, ("shard", "tensor"), None),
        P(None, ("shard", "tensor"), None),
    )
    out_specs = (
        P(None, "shard", "tensor"),
        P(None, "shard", "tensor"),
        P(None, "shard", "tensor"),
        P(None, ("shard", "tensor"), None),
        P(None, ("shard", "tensor"), None),
        P(None, ("shard", "tensor"), None),
        P(None, ("shard", "tensor"), None),
        P(None, ("shard", "tensor"), None),
        P(None, ("shard", "tensor"), None),
        P(),
    )
    return jax.shard_map(shards, mesh=mesh, in_specs=in_specs, out_specs=out_specs, check_vma=False)
```
